512 devices in a mesh: lat: 4 (over z_hi), lon: 4 (over x), day: 32 (over z_lo, y, core).
Axes of the slice: x: 4, y: 8, z: 8 (z_hi: 4, z_lo: 2; z = z_hi * 2 + z_lo), core: 2. Of those that a mesh axis runs over, the one named last changes fastest.
Arguments:
- anomaly: float32 [256, 256, 4096], P('lat', 'lon', 'day'), may hold values from -6 to 6
- observed: int32 [256, 256, 4096], P('lat', 'lon', 'day'), may hold values 0 or 1
- ocean_mask: int32 [256, 256], P('lat', 'lon'), may hold values 0 or 1
- start_days: float32 [4096, 128], P('day'), may hold values from -0.09375 to 0.09375
Outputs:
- spatial: float32 [256, 256, 128], P('lat', 'lon')
- temporal: float32 [4096, 128], P('day')
The draws below stay inside these ranges and needn't reach their ends.
Inputs may be any that keep to these rules, and one draw needn't show every extreme that they name: 1 marks an observed value, 0 a gap. `ocean_mask`: 1 marks ocean, 0 land.
All inputs are finite; a program needn't handle non-finite values. No bound on the sum of `observed` or of `ocean_mask` on one device may be relied on, other than what follows from the above.
Results may differ from the reference program's by a relative error of at most 0.0003.
Values sent between devices are 32-bit elements; how exact they have to be, the bound alone decides.
No kernel may reach another device: no remote copies, remote signals or barrier semaphores. Data moves between devices by JAX's collectives and lax.ppermute only.
A program may use at most 64 MiB of HBM per device.

```python
import math
import jax
import jax.numpy as jnp
from jax import lax

K = 128
ITERS = 2
NLAT = 256
NLON = 256
DAYS = 4096


def place_ends(array, rng, low, largest):
    longest = array.shape.index(max(array.shape))
    spots = []
    for shift in (0, 1):
        where = [jax.random.randint(jax.random.fold_in(rng, axis), (), 0, length) for axis, length in enumerate(array.shape)]
        where[longest] = (where[longest] + shift) % array.shape[longest]
        spots.append(tuple(where))
    return array.at[spots[0]].set(low).at[spots[1]].set(largest)


def level_of(rng, shape, cuts, least, high):
    def one(dim, shards_of):
        steps = jax.random.uniform(jax.random.fold_in(jax.random.fold_in(rng, 6), dim), (shards_of,), jnp.float32, least / len(cuts), high / len(cuts))
        return jnp.repeat(jnp.exp(steps), shape[dim] // shards_of).reshape((-1,) + (1,) * (len(shape) - dim - 1))

    gain = one(*cuts[0])
    for cut in cuts[1:]:
        gain = gain * one(*cut)
    return gain


def noise(key, extent, width, reach, cuts=(), kind=jnp.bfloat16):
    level = level_of(key, extent, cuts, -0.22, 0.18) if cuts else 1.0
    result = jax.random.normal(key, extent, jnp.float32) * width * level
    return jnp.minimum(jnp.maximum(result, -reach), reach).astype(kind)


def setup_inputs(seed: int = 0) -> dict:
    key_of = jax.random.split(jax.random.key(seed), 5)
    anomaly = noise(key_of[0], (NLAT, NLON, DAYS), 1.0, 6.0, ((0, 4), (1, 4), (2, 32)), jnp.float32)
    observed = place_ends((jax.random.randint(key_of[1], (NLAT, NLON, DAYS), 0, 10) < 7).astype(jnp.int32), jax.random.fold_in(key_of[1], 1), 0, 1)
    ocean_mask = place_ends((jax.random.randint(key_of[2], (NLAT, NLON), 0, 10) < 9).astype(jnp.int32), jax.random.fold_in(key_of[2], 1), 0, 1)
    start_days = noise(key_of[3], (DAYS, K), DAYS ** -0.5, 0.09375, ((0, 32),), jnp.float32)
    return dict(anomaly=anomaly, observed=observed, ocean_mask=ocean_mask, start_days=start_days)


ridge_term = 1.0
diffusion = 0.1
lat_south = 30.0
lat_span = 16.0

def product(left, right):
    return jnp.dot(left.astype(jnp.float32), right.astype(jnp.float32), precision=lax.Precision.HIGHEST, preferred_element_type=jnp.float32)

def product_tn(left, right):
    return lax.dot_general(left.astype(jnp.float32), right.astype(jnp.float32), (((0,), (0,)), ((), ())), precision=lax.Precision.HIGHEST, preferred_element_type=jnp.float32)

def product_nt(left, right):
    return lax.dot_general(left.astype(jnp.float32), right.astype(jnp.float32), (((1,), (1,)), ((), ())), precision=lax.Precision.HIGHEST, preferred_element_type=jnp.float32)

def invert(gram):
    size_k = gram.shape[0]
    identity_k = jnp.eye(size_k, dtype=jnp.float32)
    factor = jnp.linalg.cholesky(gram + ridge_term * identity_k)
    return jax.scipy.linalg.cho_solve((factor, True), identity_k)

def lat_weights(first_row, row_count, total_rows):
    index_rows = first_row + jnp.arange(row_count, dtype=jnp.float32)
    angle = (lat_south + lat_span * (index_rows + 0.5) / total_rows) * (math.pi / 180.0)
    cosine = jnp.cos(angle)
    return 1.0 / (cosine * cosine)

def smooth(modes, sea, rim_modes, sea_rim, lat_weight):
    north_south = sea_rim[:-2, 1:-1, None] * (rim_modes[:-2, 1:-1] - modes) + sea_rim[2:, 1:-1, None] * (rim_modes[2:, 1:-1] - modes)
    east_west = sea_rim[1:-1, :-2, None] * (rim_modes[1:-1, :-2] - modes) + sea_rim[1:-1, 2:, None] * (rim_modes[1:-1, 2:] - modes)
    return sea[:, :, None] * (modes + diffusion * (north_south + lat_weight[:, None, None] * east_west))

def reference(anomaly, observed, ocean_mask, start_days):
    cell_count = NLAT * NLON
    values = anomaly.reshape(cell_count, DAYS)
    seen_rows = observed.reshape(cell_count, DAYS).astype(jnp.float32)
    sea_grid = ocean_mask.astype(jnp.float32)
    sea_column = sea_grid.reshape(cell_count, 1)
    known = sea_column * seen_rows * values
    gap_weight = sea_column * (1.0 - seen_rows)
    sea_rim = jnp.pad(sea_grid, 1)
    lat_weight = lat_weights(0.0, NLAT, float(NLAT))
    temporal = start_days
    spatial = jnp.zeros((cell_count, K), jnp.float32)
    for sweep in range(ITERS):
        if sweep == 0:
            filled = known
        else:
            filled = known + gap_weight * product_nt(spatial, temporal)
        inverse_days = invert(product_tn(temporal, temporal))
        raw_modes = product(product(filled, temporal), inverse_days).reshape(NLAT, NLON, K)
        rim_modes = jnp.pad(raw_modes, ((1, 1), (1, 1), (0, 0)))
        spatial = smooth(raw_modes, sea_grid, rim_modes, sea_rim, lat_weight).reshape(cell_count, K)
        filled = known + gap_weight * product_nt(spatial, temporal)
        inverse_modes = invert(product_tn(spatial, spatial))
        temporal = product(product_tn(filled, spatial), inverse_modes)
    return (spatial.reshape(NLAT, NLON, K), temporal)
```

```python
import math

import jax
import jax.numpy as jnp
from jax import lax
from jax.sharding import Mesh, PartitionSpec as P

ITERS = 2


ridge_term = 1.0
diffusion = 0.1
lat_south = 30.0
lat_span = 16.0

YZ = ("zlo", "y")
DAY = ("zlo", "y", "core")
ALL = ("lat", "lon", "zlo", "y", "core")
LL = ("lat", "lon")


def product(left, right):
    return jnp.dot(left, right, precision=lax.Precision.HIGHEST, preferred_element_type=jnp.float32)


def product_tn(left, right):
    return lax.dot_general(
        left,
        right,
        (((0,), (0,)), ((), ())),
        precision=lax.Precision.HIGHEST,
        preferred_element_type=jnp.float32,
    )


def product_nt(left, right):
    return lax.dot_general(
        left,
        right,
        (((1,), (1,)), ((), ())),
        precision=lax.Precision.HIGHEST,
        preferred_element_type=jnp.float32,
    )


def invert(gram):
    size_k = gram.shape[0]
    identity_k = jnp.eye(size_k, dtype=jnp.float32)
    factor = jnp.linalg.cholesky(gram + ridge_term * identity_k)
    return jax.scipy.linalg.cho_solve((factor, True), identity_k)


def lat_weights(first_row, row_count, total_rows):
    index_rows = first_row + jnp.arange(row_count, dtype=jnp.float32)
    angle = (lat_south + lat_span * (index_rows + 0.5) / total_rows) * (math.pi / 180.0)
    cosine = jnp.cos(angle)
    return 1.0 / (cosine * cosine)


def swap_core(value):
    return lax.ppermute(value, "core", [(0, 1), (1, 0)])


def halo_pairs(lats, lons, spokes):
    pairs = []
    for la in range(lats):
        for lo in range(lons):
            for q in range(spokes):
                for core in range(2):
                    step = -1 if q < spokes // 2 else 1
                    to_la, to_lo = (la + step, lo) if core == 0 else (la, lo + step)
                    if 0 <= to_la < lats and 0 <= to_lo < lons:
                        here = ((la * lons + lo) * spokes + q) * 2 + core
                        there = ((to_la * lons + to_lo) * spokes + q) * 2 + core
                        pairs.append((here, there))
    return pairs


def gather_all(value, axes, size):
    spread = jnp.broadcast_to(value[None], (size,) + value.shape)
    return lax.all_to_all(spread, axes, 0, 0, tiled=True)


def sum_cells(value):
    size = lax.axis_size("lat") * lax.axis_size("lon")
    rows = value.shape[0]
    parts = lax.all_to_all(value.reshape(size, rows // size, -1), LL, 0, 0, tiled=True)
    mine = jnp.sum(parts, axis=0)
    return gather_all(mine, LL, size).reshape(rows, -1)


def edges_of(grid):
    return jnp.concatenate([grid[0], grid[-1], grid[:, 0], grid[:, -1]], axis=0)


def on_device(anomaly, observed, ocean_mask, start_days):
    rows_lat, cols_lon, days_dev = anomaly.shape
    rank_count = start_days.shape[1]
    cell_count = rows_lat * cols_lon
    lats, lons = lax.axis_size("lat"), lax.axis_size("lon")
    spokes = lax.axis_size("zlo") * lax.axis_size("y")
    core = lax.axis_index("core")
    spoke = lax.axis_index("zlo") * lax.axis_size("y") + lax.axis_index("y")
    pairs = halo_pairs(lats, lons, spokes)
    chunk = cell_count // (2 * spokes)
    values = anomaly.reshape(cell_count, days_dev)
    seen_rows = observed.reshape(cell_count, days_dev).astype(jnp.float32)
    sea_grid = ocean_mask.astype(jnp.float32)
    sea_column = sea_grid.reshape(cell_count, 1)
    known = sea_column * seen_rows * values
    gap_weight = sea_column * (1.0 - seen_rows)
    first_lat = (lax.axis_index("lat") * rows_lat).astype(jnp.float32)
    lat_weight = lat_weights(first_lat, rows_lat, float(rows_lat * lats))[:, None]
    edge_sea = edges_of(sea_grid).reshape(2, spokes, 1, 8)
    edge_sea = jnp.pad(edge_sea, ((0, 0), (0, 0), (0, 7), (0, rank_count - 8)))
    edge_sea = lax.dynamic_index_in_dim(edge_sea, core, 0, False)
    edge_sea = lax.dynamic_index_in_dim(edge_sea, spoke, 0, False)
    temporal = start_days
    spatial = jnp.zeros((cell_count, rank_count), jnp.float32)
    around = None
    for sweep in range(ITERS):
        if sweep == 0:
            filled = known
        else:
            filled = known + gap_weight * product_nt(spatial, temporal)
        partial = product(filled, temporal)
        gram = product_tn(temporal, temporal)
        block = jnp.concatenate(
            [
                partial.reshape(2, spokes, chunk, rank_count),
                edges_of(partial.reshape(rows_lat, cols_lon, rank_count)).reshape(2, spokes, 8, rank_count),
                gram.reshape(2, spokes, 4, rank_count),
                jnp.zeros((2, spokes, 4, rank_count), jnp.float32),
            ],
            axis=2,
        )
        mine = lax.dynamic_index_in_dim(block, core, 0, False)
        other = lax.dynamic_index_in_dim(block, 1 - core, 0, False)
        half = mine + swap_core(other)
        shard = jnp.sum(lax.all_to_all(half, YZ, 0, 0, tiled=True), axis=0)
        send = shard[chunk : chunk + 8]
        if sweep == 0:
            send = jnp.concatenate([send, edge_sea], axis=0)
        halo = lax.ppermute(send, ALL, pairs)
        sea_rows = halo[8:12] if sweep == 0 else jnp.zeros((4, rank_count), jnp.float32)
        shard = jnp.concatenate([shard[:chunk], halo[:8], shard[chunk + 8 : chunk + 12], sea_rows], axis=0)
        here = gather_all(shard, YZ, spokes)
        there = swap_core(here)
        full = jnp.where(core == 0, jnp.stack([here, there]), jnp.stack([there, here]))
        raw = full[:, :, :chunk].reshape(rows_lat, cols_lon, rank_count)
        rims = full[:, :, chunk : chunk + 8].reshape(4, rows_lat, rank_count)
        gram_days = full[:, :, chunk + 8 : chunk + 12].reshape(rank_count, rank_count)
        if sweep == 0:
            rim_sea = full[:, :, chunk + 12, :8].reshape(4, rows_lat)
            sea_ns = jnp.concatenate([rim_sea[1][None], sea_grid, rim_sea[0][None]], axis=0)
            sea_we = jnp.concatenate([rim_sea[3][:, None], sea_grid, rim_sea[2][:, None]], axis=1)
            around = 1.0 - diffusion * (
                sea_ns[:-2] + sea_ns[2:] + lat_weight * (sea_we[:, :-2] + sea_we[:, 2:])
            )
        raw_ns = jnp.concatenate([rims[1][None], raw, rims[0][None]], axis=0)
        raw_we = jnp.concatenate([rims[3][:, None], raw, rims[2][:, None]], axis=1)
        smoothed = sea_grid[:, :, None] * (
            around[:, :, None] * raw
            + diffusion
            * (raw_ns[:-2] + raw_ns[2:] + lat_weight[:, :, None] * (raw_we[:, :-2] + raw_we[:, 2:]))
        )
        spatial = product(smoothed.reshape(cell_count, rank_count), invert(gram_days))
        filled = known + gap_weight * product_nt(spatial, temporal)
        projected = product_tn(filled, spatial)
        sums = sum_cells(jnp.concatenate([projected, product_tn(spatial, spatial)], axis=0))
        temporal = product(sums[:days_dev], invert(sums[days_dev:]))
    return (spatial.reshape(rows_lat, cols_lon, rank_count), temporal)


def solution(mesh):
    lats, lons, days = mesh.devices.shape
    fine = Mesh(mesh.devices.reshape(lats, lons, 2, days // 4, 2), ALL)
    in_specs = (P("lat", "lon", DAY), P("lat", "lon", DAY), P("lat", "lon"), P(DAY, None))
    out_specs = (P("lat", "lon", None), P(DAY, None))
    return jax.shard_map(
        on_device, mesh=fine, in_specs=in_specs, out_specs=out_specs, check_vma=False
    )
```

```python
import functools
import math

import jax
import jax.numpy as jnp
from jax import lax
from jax.experimental import pallas as pl
from jax.experimental.pallas import tpu as pltpu
from jax.sharding import Mesh, PartitionSpec as P

ITERS = 2


ridge_term = 1.0
diffusion = 0.1
lat_south = 30.0
lat_span = 16.0

GAP = 1e30
YZ = ("zlo", "y")
DAY = ("zlo", "y", "core")
ALL = ("lat", "lon", "zlo", "y", "core")
LL = ("lat", "lon")
f32, bf16 = jnp.float32, jnp.bfloat16


def inverse_spd(matrix):
    size = matrix.shape[0]
    blocks = [matrix[8 * r : 8 * r + 8] for r in range(size // 8)]
    lane = lax.broadcasted_iota(jnp.int32, (1, size), 1)
    row = lax.broadcasted_iota(jnp.int32, (8, size), 0)
    for k in range(0, size, 4):
        home, off = k // 8, k % 8
        rows = [blocks[home][off + i : off + i + 1] for i in range(4)]
        d = [[jnp.broadcast_to(rows[i][:, k + j : k + j + 1], (1, size)) for j in range(4)] for i in range(4)]
        in_panel = (lane >= k) & (lane < k + 4)
        a, b, c = d[0][0], d[0][1], d[1][1]
        r = 1.0 / (a * c - b * b)
        a00, a01, a11 = c * r, -b * r, a * r
        b02, b03, b12, b13 = d[0][2], d[0][3], d[1][2], d[1][3]
        g02, g03 = a00 * b02 + a01 * b12, a00 * b03 + a01 * b13
        g12, g13 = a01 * b02 + a11 * b12, a01 * b03 + a11 * b13
        s22 = d[2][2] - (b02 * g02 + b12 * g12)
        s23 = d[2][3] - (b02 * g03 + b12 * g13)
        s33 = d[3][3] - (b03 * g03 + b13 * g13)
        r = 1.0 / (s22 * s33 - s23 * s23)
        i22, i23, i33 = s33 * r, -s23 * r, s22 * r
        h02, h03 = g02 * i22 + g03 * i23, g02 * i23 + g03 * i33
        h12, h13 = g12 * i22 + g13 * i23, g12 * i23 + g13 * i33
        q00 = a00 + (h02 * g02 + h03 * g03)
        q01 = a01 + (h02 * g12 + h03 * g13)
        q11 = a11 + (h12 * g12 + h13 * g13)
        inv = [[q00, q01, -h02, -h03], [q01, q11, -h12, -h13], [-h02, -h12, i22, i23], [-h03, -h13, i23, i33]]
        unit = [jnp.where(lane == k + j, 1.0, jnp.where(in_panel, 0.0, rows[j])) for j in range(4)]
        new = [
            (inv[i][0] * unit[0] + inv[i][1] * unit[1]) + (inv[i][2] * unit[2] + inv[i][3] * unit[3])
            for i in range(4)
        ]
        out = []
        for r8, block in enumerate(blocks):
            cols = [block[:, k + j : k + j + 1] for j in range(4)]
            keep = jnp.where(in_panel, 0.0, block)
            keep = keep - ((cols[0] * new[0] + cols[1] * new[1]) + (cols[2] * new[2] + cols[3] * new[3]))
            if r8 == home:
                for j in range(4):
                    keep = jnp.where(row == off + j, new[j], keep)
            out.append(keep)
        blocks = out
    return jnp.concatenate(blocks, axis=0)


def add_ridge(gram):
    size = gram.shape[0]
    same = lax.broadcasted_iota(jnp.int32, (size, size), 0) == lax.broadcasted_iota(jnp.int32, (size, size), 1)
    return gram + jnp.where(same, ridge_term, 0.0)


def split(value):
    one = value.astype(bf16)
    rest = value - one.astype(f32)
    two = rest.astype(bf16)
    three = (rest - two.astype(f32)).astype(bf16)
    return one, two, three


def right_side(value):
    one, two, three = split(value)
    wide = jnp.concatenate([one, two], axis=1)
    return jnp.concatenate([wide, wide], axis=0), jnp.concatenate([three, one], axis=0)


def times(parts, side):
    one, two, three = parts
    wide = jnp.dot(jnp.concatenate([one, two], axis=1), side[0], preferred_element_type=f32)
    tail = jnp.dot(jnp.concatenate([one, three], axis=1), side[1], preferred_element_type=f32)
    n = tail.shape[1]
    return wide[:, :n] + (wide[:, n:] + tail)


def dot_tn(left, right):
    return lax.dot_general(left, right, (((0,), (0,)), ((), ())), preferred_element_type=f32)


def full(left, right, dims=(((1,), (0,)), ((), ()))):
    return lax.dot_general(left, right, dims, precision=lax.Precision.HIGHEST, preferred_element_type=f32)


def put_block(core_ref, grid_ref, gram, mine_ref, other_ref):
    core = core_ref[0, 0]
    lats, lons, modes = grid_ref.shape
    spokes = mine_ref.shape[0]
    per = lats // (2 * spokes)
    cells = per * lons

    def edge(half, q):
        half_spokes = spokes // 2
        at = 8 * (q % half_spokes)
        far = q >= half_spokes
        if half == 0:
            return grid_ref[lats - 1 if far else 0, at : at + 8, :]
        return grid_ref[at : at + 8, lons - 1 if far else 0, :]

    for half in range(2):
        for which, ref in ((half, mine_ref), (1 - half, other_ref)):

            @pl.when(core == which)
            def _():
                for q in range(spokes):
                    ref[q, cells : cells + 8, :] = edge(half, q)
                    ref[q, cells + 8 : cells + 16, :] = gram[8 * q : 8 * q + 8]


def first_kernel(core_ref, anomaly_ref, observed_ref, seat_ref, days_ref, mine_ref, other_ref, coded_ref, sea_ref, grid_ref):
    core = core_ref[0, 0]
    lats, lons, days = anomaly_ref.shape
    spokes = mine_ref.shape[0]
    per = lats // (2 * spokes)
    temporal = days_ref[...]
    side = right_side(temporal)
    gram = full(temporal, temporal, (((0,), (0,)), ((), ())))
    seat = seat_ref[...]

    for half, ref in ((core, mine_ref), (1 - core, other_ref)):

        def step(q, _):
            rows = []
            for p in range(per):
                i = half * (lats // 2) + q * per + p
                sea = jnp.broadcast_to(pltpu.roll(seat, lax.rem(seat.shape[1] - i, seat.shape[1]), 1)[:, :1], (lons, days))
                sea_ref[i] = sea
                seen = observed_ref[i] != 0
                known = jnp.where(seen, sea * anomaly_ref[i], 0.0)
                coded_ref[i] = jnp.where(seen | (sea == 0.0), known, GAP)
                rows.append(known)
            out = times(split(jnp.concatenate(rows, axis=0)), side)
            ref[q, 0 : per * lons, :] = out
            for p in range(per):
                grid_ref[half * (lats // 2) + q * per + p] = out[p * lons : (p + 1) * lons]
            return _

        lax.fori_loop(0, spokes, step, 0, unroll=2)
    put_block(core_ref, grid_ref, gram, mine_ref, other_ref)


def modes_kernel(first, core_ref, weight_ref, here_ref, there_ref, days_ref, coded_ref, field_ref, *refs):
    if first:
        spatial_ref, sums_ref, around_ref, pad_ref, rim_ref, wide_ref, tail_ref = refs
    else:
        spatial_ref, sums_ref, pad_ref, rim_ref, wide_ref, tail_ref = refs
    core = core_ref[0, 0]
    lats, lons, modes = coded_ref.shape
    days = modes
    spokes = here_ref.shape[0]
    per = lats // (2 * spokes)
    cells = per * lons
    tiles = 2 if first else 1
    gram_at = cells + 8 * tiles

    for half, ref in ((core, here_ref), (1 - core, there_ref)):

        def fill(q, _):
            base = half * (lats // 2) + q * per
            for p in range(per):
                pad_ref[base + p + 1] = ref[q, p * lons : (p + 1) * lons, :]
            at = half * 2 * lons + q * 8
            for t in range(tiles):
                rim_ref[pl.ds(pl.multiple_of(t * 4 * lons + at, 8), 8), :] = ref[q, cells + 8 * t : cells + 8 * t + 8, :]
            return _

        lax.fori_loop(0, spokes, fill, 0)
    pad_ref[0] = rim_ref[lons : 2 * lons, :]
    pad_ref[lats + 1] = rim_ref[0:lons, :]
    gram = jnp.concatenate([here_ref[q, gram_at : gram_at + 8, :] for q in range(spokes)], axis=0)
    inverse_side = right_side(inverse_spd(add_ridge(gram)))
    days_side = right_side(days_ref[...].T)
    row = lax.broadcasted_iota(jnp.int32, (lons, modes), 0)
    wide_ref[...] = jnp.zeros_like(wide_ref)
    tail_ref[...] = jnp.zeros_like(tail_ref)

    def beside(value, i, kind):
        east = rim_ref[pl.ds(kind * 4 * lons + 2 * lons + i, 1), :]
        west = rim_ref[pl.ds(kind * 4 * lons + 3 * lons + i, 1), :]
        ahead = jnp.where(row == lons - 1, east, pltpu.roll(value, lons - 1, 0))
        behind = jnp.where(row == 0, west, pltpu.roll(value, 1, 0))
        return ahead + behind

    if first:

        def masks(i, _):
            sea = field_ref[i]
            north = jnp.where(i == 0, rim_ref[5 * lons : 6 * lons, :], field_ref[jnp.maximum(i - 1, 0)])
            south = jnp.where(i == lats - 1, rim_ref[4 * lons : 5 * lons, :], field_ref[jnp.minimum(i + 1, lats - 1)])
            round_ = (north + south) + weight_ref[0, i] * beside(sea, i, 1)
            around_ref[i] = jnp.where(sea == 0.0, GAP, 1.0 - diffusion * round_)
            return _

        lax.fori_loop(0, lats, masks, 0)
    around_in = around_ref if first else field_ref

    group = 4

    def step(g, _):
        smoothed = []
        for p in range(group):
            i = g * group + p
            around = around_in[i]
            raw = pad_ref[i + 1]
            near = (pad_ref[i] + pad_ref[i + 2]) + weight_ref[0, i] * beside(raw, i, 0)
            smoothed.append(jnp.where(around == GAP, 0.0, around * raw + diffusion * near))
        spatial = times(split(jnp.concatenate(smoothed, axis=0)), inverse_side)
        parts = split(spatial)
        guess = times(parts, days_side)
        filled = []
        for p in range(group):
            i = g * group + p
            spatial_ref[i] = spatial[p * lons : (p + 1) * lons]
            coded = coded_ref[i]
            filled.append(jnp.where(coded == GAP, guess[p * lons : (p + 1) * lons], coded))
        f1, f2, f3 = split(jnp.concatenate(filled, axis=0))
        s1, s2, s3 = parts
        wide_ref[...] += dot_tn(jnp.concatenate([f1, f2, s1, s2], axis=1), jnp.concatenate([s1, s2], axis=1))
        tail_ref[...] += dot_tn(
            jnp.concatenate([jnp.concatenate([f1, s1], axis=1), jnp.concatenate([f3, s3], axis=1)], axis=0),
            jnp.concatenate([s3, s1], axis=0),
        )
        return _

    lax.fori_loop(0, lats // group, step, 0)
    n = modes
    for part in range(2):
        at = 2 * part * n
        wide = wide_ref[at : at + n, :] + wide_ref[at + n : at + 2 * n, :]
        sums_ref[part * n : (part + 1) * n, :] = (wide[:, :n] + wide[:, n:]) + tail_ref[part * n : (part + 1) * n, :]


def days_kernel(core_ref, sums_ref, coded_ref, spatial_ref, mine_ref, other_ref, days_ref, grid_ref):
    core = core_ref[0, 0]
    lats, lons, modes = coded_ref.shape
    days = sums_ref.shape[0] - modes
    spokes = mine_ref.shape[0]
    per = lats // (2 * spokes)
    temporal = full(sums_ref[0:days, :], inverse_spd(add_ridge(sums_ref[days:, :])))
    days_ref[...] = temporal
    side = right_side(temporal)
    across = right_side(temporal.T)
    gram = full(temporal, temporal, (((0,), (0,)), ((), ())))

    for half, ref in ((core, mine_ref), (1 - core, other_ref)):

        def step(q, _):
            base = half * (lats // 2) + q * per
            guess = times(split(jnp.concatenate([spatial_ref[base + p] for p in range(per)], axis=0)), across)
            coded = jnp.concatenate([coded_ref[base + p] for p in range(per)], axis=0)
            out = times(split(jnp.where(coded == GAP, guess, coded)), side)
            ref[q, 0 : per * lons, :] = out
            for p in range(per):
                grid_ref[base + p] = out[p * lons : (p + 1) * lons]
            return _

        lax.fori_loop(0, spokes, step, 0, unroll=2)
    put_block(core_ref, grid_ref, gram, mine_ref, other_ref)


def last_kernel(sums_ref, days_ref):
    days = days_ref.shape[0]
    days_ref[...] = full(sums_ref[0:days, :], inverse_spd(add_ridge(sums_ref[days:, :])))


SMEM = pl.BlockSpec(memory_space=pltpu.SMEM)
VMEM = pl.BlockSpec(memory_space=pltpu.VMEM)


def call(kernel, outs, specs, scratch, name, flops, nbytes):
    return pl.pallas_call(
        kernel,
        out_shape=[jax.ShapeDtypeStruct(shape, f32) for shape in outs],
        in_specs=specs,
        out_specs=[VMEM] * len(outs),
        scratch_shapes=[pltpu.VMEM(shape, f32) for shape in scratch],
        name=name,
        cost_estimate=pl.CostEstimate(flops=flops, bytes_accessed=nbytes, transcendentals=0),
        compiler_params=pltpu.CompilerParams(vmem_limit_bytes=40 * 1024 * 1024),
    )


def first_call(core, anomaly, observed, seat, days, spokes):
    lats, lons, n = anomaly.shape
    block = (spokes, lats * lons // (2 * spokes) + 16, n)
    grid = (lats, lons, n)
    return call(first_kernel, [block, block, grid, grid], [SMEM] + [VMEM] * 4, [grid], "first_projection", 10**9, 10**7)(
        core, anomaly, observed, seat, days
    )


def modes_call(first, core, weight, here, there, days, coded, field):
    lats, lons, n = coded.shape
    grid = (lats, lons, n)
    outs = [grid, (2 * n, n)] + ([grid] if first else [])
    scratch = [(lats + 2, lons, n), ((8 if first else 4) * lons, n), (4 * n, 2 * n), (2 * n, n)]
    return call(functools.partial(modes_kernel, first), outs, [SMEM, SMEM] + [VMEM] * 5, scratch, "modes_sweep", 2 * 10**9, 10**7)(
        core, weight, here, there, days, coded, field
    )


def days_call(core, sums, coded, spatial, spokes):
    lats, lons, n = coded.shape
    block = (spokes, lats * lons // (2 * spokes) + 16, n)
    return call(days_kernel, [block, block, (sums.shape[0] - n, n)], [SMEM] + [VMEM] * 3, [(lats, lons, n)], "days_sweep", 2 * 10**9, 10**7)(
        core, sums, coded, spatial
    )


def last_call(sums):
    n = sums.shape[1]
    return call(last_kernel, [(sums.shape[0] - n, n)], [VMEM], [], "last_days", 10**7, 10**6)(sums)[0]


def lat_weights(first_row, row_count, total_rows):
    index_rows = first_row + jnp.arange(row_count, dtype=jnp.float32)
    angle = (lat_south + lat_span * (index_rows + 0.5) / total_rows) * (math.pi / 180.0)
    cosine = jnp.cos(angle)
    return 1.0 / (cosine * cosine)


def swap_core(value):
    return lax.ppermute(value, "core", [(0, 1), (1, 0)])


def halo_pairs(lats, lons, spokes):
    pairs = []
    for la in range(lats):
        for lo in range(lons):
            for q in range(spokes):
                for core in range(2):
                    step = -1 if q < spokes // 2 else 1
                    to_la, to_lo = (la + step, lo) if core == 0 else (la, lo + step)
                    if 0 <= to_la < lats and 0 <= to_lo < lons:
                        here = ((la * lons + lo) * spokes + q) * 2 + core
                        there = ((to_la * lons + to_lo) * spokes + q) * 2 + core
                        pairs.append((here, there))
    return pairs


def gather_all(value, axes, size):
    spread = jnp.broadcast_to(value[None], (size,) + value.shape)
    return lax.all_to_all(spread, axes, 0, 0, tiled=True)


def sum_cells(value):
    size = lax.axis_size("lat") * lax.axis_size("lon")
    rows = value.shape[0]
    parts = lax.all_to_all(value.reshape(size, rows // size, -1), LL, 0, 0, tiled=True)
    mine = jnp.sum(parts, axis=0)
    return gather_all(mine, LL, size).reshape(rows, -1)


def edges_of(grid):
    return jnp.concatenate([grid[0], grid[-1], grid[:, 0], grid[:, -1]], axis=0)


def on_device(anomaly, observed, ocean_mask, start_days):
    rows_lat, cols_lon, _ = anomaly.shape
    rank_count = start_days.shape[1]
    lats, lons = lax.axis_size("lat"), lax.axis_size("lon")
    spokes = lax.axis_size("zlo") * lax.axis_size("y")
    core = lax.axis_index("core")
    spoke = lax.axis_index("zlo") * lax.axis_size("y") + lax.axis_index("y")
    pairs = halo_pairs(lats, lons, spokes)
    cells = rows_lat * cols_lon // (2 * spokes)
    core_word = core.reshape(1, 1).astype(jnp.int32)
    sea_grid = ocean_mask.astype(f32)
    seat = jnp.pad(sea_grid.T, ((0, 0), (0, rank_count - rows_lat)))
    first_lat = (lax.axis_index("lat") * rows_lat).astype(f32)
    weight = lat_weights(first_lat, rows_lat, float(rows_lat * lats)).reshape(1, rows_lat)
    edge_sea = lax.dynamic_slice_in_dim(edges_of(sea_grid), (core * spokes + spoke) * 8, 8)
    edge_sea = jnp.broadcast_to(edge_sea[:, None], (8, rank_count))
    temporal = start_days
    mine, other, coded, field = first_call(core_word, anomaly, observed, seat, start_days, spokes)
    for sweep in range(ITERS):
        half = mine + swap_core(other)
        shard = jnp.sum(lax.all_to_all(half, YZ, 0, 0, tiled=True), axis=0)
        send = shard[cells : cells + 8]
        if sweep == 0:
            send = jnp.concatenate([send, edge_sea], axis=0)
        halo = lax.ppermute(send, ALL, pairs)
        shard = jnp.concatenate([shard[:cells], halo, shard[cells + 8 :]], axis=0)
        here = gather_all(shard, YZ, spokes)
        there = swap_core(here)
        out = modes_call(sweep == 0, core_word, weight, here, there, temporal, coded, field)
        spatial, sums = out[0], sum_cells(out[1])
        if sweep == 0:
            field = out[2]
        if sweep < ITERS - 1:
            mine, other, temporal = days_call(core_word, sums, coded, spatial, spokes)
        else:
            temporal = last_call(sums)
    return (spatial, temporal)


def solution(mesh):
    lats, lons, days = mesh.devices.shape
    fine = Mesh(mesh.devices.reshape(lats, lons, 2, days // 4, 2), ALL)
    in_specs = (P("lat", "lon", DAY), P("lat", "lon", DAY), P("lat", "lon"), P(DAY, None))
    out_specs = (P("lat", "lon", None), P(DAY, None))
    return jax.shard_map(
        on_device, mesh=fine, in_specs=in_specs, out_specs=out_specs, check_vma=False
    )
```

```python
import functools
import math

import jax
import jax.numpy as jnp
from jax import lax
from jax.experimental import pallas as pl
from jax.experimental.pallas import tpu as pltpu
from jax.sharding import Mesh, PartitionSpec as P

ITERS = 2


ridge_term = 1.0
diffusion = 0.1
lat_south = 30.0
lat_span = 16.0

GAP = 1e30
PIECES = 8
GROUP = 16
YZ = ("zlo", "y")
DAY = ("zlo", "y", "core")
ALL = ("lat", "lon", "zlo", "y", "core")
LL = ("lat", "lon")
f32, bf16 = jnp.float32, jnp.bfloat16


def inverse_spd(matrix):
    size = matrix.shape[0]
    blocks = [matrix[8 * r : 8 * r + 8] for r in range(size // 8)]
    lane = lax.broadcasted_iota(jnp.int32, (1, size), 1)
    row = lax.broadcasted_iota(jnp.int32, (8, size), 0)
    for k in range(0, size, 4):
        home, off = k // 8, k % 8
        rows = [blocks[home][off + i : off + i + 1] for i in range(4)]
        d = [[jnp.broadcast_to(rows[i][:, k + j : k + j + 1], (1, size)) for j in range(4)] for i in range(4)]
        in_panel = (lane >= k) & (lane < k + 4)
        a, b, c = d[0][0], d[0][1], d[1][1]
        r = 1.0 / (a * c - b * b)
        a00, a01, a11 = c * r, -b * r, a * r
        b02, b03, b12, b13 = d[0][2], d[0][3], d[1][2], d[1][3]
        g02, g03 = a00 * b02 + a01 * b12, a00 * b03 + a01 * b13
        g12, g13 = a01 * b02 + a11 * b12, a01 * b03 + a11 * b13
        s22 = d[2][2] - (b02 * g02 + b12 * g12)
        s23 = d[2][3] - (b02 * g03 + b12 * g13)
        s33 = d[3][3] - (b03 * g03 + b13 * g13)
        r = 1.0 / (s22 * s33 - s23 * s23)
        i22, i23, i33 = s33 * r, -s23 * r, s22 * r
        h02, h03 = g02 * i22 + g03 * i23, g02 * i23 + g03 * i33
        h12, h13 = g12 * i22 + g13 * i23, g12 * i23 + g13 * i33
        q00 = a00 + (h02 * g02 + h03 * g03)
        q01 = a01 + (h02 * g12 + h03 * g13)
        q11 = a11 + (h12 * g12 + h13 * g13)
        inv = [[q00, q01, -h02, -h03], [q01, q11, -h12, -h13], [-h02, -h12, i22, i23], [-h03, -h13, i23, i33]]
        unit = [jnp.where(lane == k + j, 1.0, jnp.where(in_panel, 0.0, rows[j])) for j in range(4)]
        new = [
            (inv[i][0] * unit[0] + inv[i][1] * unit[1]) + (inv[i][2] * unit[2] + inv[i][3] * unit[3])
            for i in range(4)
        ]
        out = []
        for r8, block in enumerate(blocks):
            cols = [block[:, k + j : k + j + 1] for j in range(4)]
            keep = jnp.where(in_panel, 0.0, block)
            keep = keep - ((cols[0] * new[0] + cols[1] * new[1]) + (cols[2] * new[2] + cols[3] * new[3]))
            if r8 == home:
                for j in range(4):
                    keep = jnp.where(row == off + j, new[j], keep)
            out.append(keep)
        blocks = out
    return jnp.concatenate(blocks, axis=0)


def add_ridge(gram):
    size = gram.shape[0]
    same = lax.broadcasted_iota(jnp.int32, (size, size), 0) == lax.broadcasted_iota(jnp.int32, (size, size), 1)
    return gram + jnp.where(same, ridge_term, 0.0)


def split(value):
    one = value.astype(bf16)
    return jnp.concatenate([one, (value - one.astype(f32)).astype(bf16)], axis=1)


def right_side(value):
    wide = split(value)
    return jnp.concatenate([wide, wide], axis=0)


def times(parts, side):
    wide = jnp.dot(parts, side, preferred_element_type=f32)
    n = wide.shape[1] // 2
    return wide[:, :n] + wide[:, n:]


def dot_tn(left, right):
    return lax.dot_general(left, right, (((0,), (0,)), ((), ())), preferred_element_type=f32)


def full(left, right, dims=(((1,), (0,)), ((), ()))):
    return lax.dot_general(left, right, dims, precision=lax.Precision.HIGHEST, preferred_element_type=f32)


def put_block(half, grid_ref, gram_ref, ref):
    lats, lons, modes = grid_ref.shape
    spokes = ref.shape[0]
    cells = lats * lons // spokes
    line = grid_ref[half * (lats - 1)]
    for q in range(spokes):
        if q < lons // 8:
            edge = line[8 * q : 8 * q + 8]
        else:
            side, at = divmod(8 * q - lons, lats)
            edge = grid_ref[at : at + 8, side * (lons - 1), :]
        ref[q, cells : cells + 8, :] = edge
        ref[q, cells + 8 : cells + 16, :] = gram_ref[8 * q : 8 * q + 8, :]


def put_rows(ref, grid_ref, g, base, out):
    lons = grid_ref.shape[1]
    cells = ref.shape[1] - 16
    for p in range(PIECES):
        ref[g * PIECES + p, 0:cells, :] = out[p * cells : (p + 1) * cells]
    for p in range(out.shape[0] // lons):
        grid_ref[base + p] = out[p * lons : (p + 1) * lons]


def first_kernel(mine, core_ref, anomaly_ref, observed_ref, seat_ref, days_ref, ref, coded_ref, sea_ref, grid_ref, gram_ref):
    core = core_ref[0, 0]
    half = core if mine else 1 - core
    lats, lons, days = coded_ref.shape
    spokes = ref.shape[0]
    many = PIECES * lats // spokes
    temporal = days_ref[...]
    side = right_side(temporal)
    gram_ref[...] = full(temporal, temporal, (((0,), (0,)), ((), ())))
    seat = seat_ref[...]

    def step(g, _):
        rows = []
        for p in range(many):
            here = g * many + p
            i = half * lats + here
            sea = jnp.broadcast_to(pltpu.roll(seat, lax.rem(seat.shape[1] - i, seat.shape[1]), 1)[:, :1], (lons, days))
            sea_ref[here] = sea
            seen = observed_ref[i] != 0
            known = jnp.where(seen, sea * anomaly_ref[i], 0.0)
            coded_ref[here] = jnp.where(seen | (sea == 0.0), known, GAP)
            rows.append(known)
        put_rows(ref, grid_ref, g, g * many, times(split(jnp.concatenate(rows, axis=0)), side))
        return _

    lax.fori_loop(0, spokes // PIECES, step, 0)
    put_block(half, grid_ref, gram_ref, ref)


def modes_kernel(first, core_ref, weight_ref, here_ref, there_ref, days_ref, *refs):
    coded_refs, field_refs, refs = refs[0:2], refs[2:4], refs[4:]
    spatial_ref, sums_ref = refs[0:2]
    around_refs = refs[2:4] if first else field_refs
    pad_ref, rim_ref, wide_ref = refs[-3:]
    core = core_ref[0, 0]
    lats, lons, modes = spatial_ref.shape
    deep = lats // 2
    spokes = here_ref.shape[0]
    per = deep // spokes
    cells = per * lons
    tiles = 2 if first else 1
    gram_at = cells + 8 * tiles
    halves = (core, 1 - core)

    for half, ref in zip(halves, (here_ref, there_ref)):
        for q in range(spokes):
            for p in range(per):
                pad_ref[half * deep + q * per + p + 1] = ref[q, p * lons : (p + 1) * lons, :]
            if q < lons // 8:
                at = half * lons + 8 * q
            else:
                side, along = divmod(8 * q - lons, deep)
                at = 2 * lons + side * lats + half * deep + along
            for t in range(tiles):
                rim_ref[pl.ds(pl.multiple_of(t * 4 * lons + at, 8), 8), :] = ref[q, cells + 8 * t : cells + 8 * t + 8, :]
    pad_ref[0] = rim_ref[lons : 2 * lons, :]
    pad_ref[lats + 1] = rim_ref[0:lons, :]
    gram = jnp.concatenate([here_ref[q, gram_at : gram_at + 8, :] for q in range(spokes)], axis=0)
    inverse_side = right_side(inverse_spd(add_ridge(gram)))
    days_side = right_side(days_ref[...].T)
    row = lax.broadcasted_iota(jnp.int32, (lons, modes), 0)

    def beside(value, i, kind):
        east = rim_ref[pl.ds(kind * 4 * lons + 2 * lons + i, 1), :]
        west = rim_ref[pl.ds(kind * 4 * lons + 2 * lons + lats + i, 1), :]
        ahead = jnp.where(row == lons - 1, east, pltpu.roll(value, lons - 1, 0))
        behind = jnp.where(row == 0, west, pltpu.roll(value, 1, 0))
        return ahead + behind

    if first:
        for n, half in enumerate(halves):
            field_ref, beyond_ref, around_ref = field_refs[n], field_refs[1 - n], around_refs[n]

            def masks(l, _, half=half, field_ref=field_ref, beyond_ref=beyond_ref, around_ref=around_ref):
                i = half * deep + l
                sea = field_ref[l]
                above = jnp.where(half == 0, rim_ref[5 * lons : 6 * lons, :], beyond_ref[deep - 1])
                below = jnp.where(half == 0, beyond_ref[0], rim_ref[4 * lons : 5 * lons, :])
                north = jnp.where(l == 0, above, field_ref[jnp.maximum(l - 1, 0)])
                south = jnp.where(l == deep - 1, below, field_ref[jnp.minimum(l + 1, deep - 1)])
                round_ = (north + south) + weight_ref[0, i] * beside(sea, i, 1)
                around_ref[l] = jnp.where(sea == 0.0, GAP, 1.0 - diffusion * round_)
                return _

            lax.fori_loop(0, deep, masks, 0, unroll=2)

    wide_ref[...] = jnp.zeros_like(wide_ref)
    for n, half in enumerate(halves):

        def step(g, _, half=half, around_ref=around_refs[n], coded_ref=coded_refs[n]):
            smoothed = []
            for p in range(GROUP):
                l = g * GROUP + p
                i = half * deep + l
                around = around_ref[l]
                raw = pad_ref[i + 1]
                near = (pad_ref[i] + pad_ref[i + 2]) + weight_ref[0, i] * beside(raw, i, 0)
                smoothed.append(jnp.where(around == GAP, 0.0, around * raw + diffusion * near))
            spatial = times(split(jnp.concatenate(smoothed, axis=0)), inverse_side)
            parts = split(spatial)
            guess = times(parts, days_side)
            filled = []
            for p in range(GROUP):
                l = g * GROUP + p
                spatial_ref[half * deep + l] = spatial[p * lons : (p + 1) * lons]
                coded = coded_ref[l]
                filled.append(jnp.where(coded == GAP, guess[p * lons : (p + 1) * lons], coded))
            filled = split(jnp.concatenate(filled, axis=0))
            wide_ref[...] += dot_tn(jnp.concatenate([filled, parts], axis=1), parts)
            return _

        lax.fori_loop(0, deep // GROUP, step, 0)
    m = modes
    for part in range(2):
        at = 2 * part * m
        wide = wide_ref[at : at + m, :] + wide_ref[at + m : at + 2 * m, :]
        sums_ref[part * m : (part + 1) * m, :] = wide[:, :m] + wide[:, m:]


def days_kernel(mine, core_ref, sums_ref, coded_ref, spatial_ref, ref, *refs):
    core = core_ref[0, 0]
    half = core if mine else 1 - core
    grid_ref, gram_ref = refs[-2:]
    lats, lons, modes = coded_ref.shape
    spokes = ref.shape[0]
    many = PIECES * lats // spokes
    if mine:
        temporal = sums_ref[...]
    else:
        days = sums_ref.shape[0] - modes
        temporal = full(sums_ref[0:days, :], inverse_spd(add_ridge(sums_ref[days:, :])))
        refs[0][...] = temporal
    side = right_side(temporal)
    across = right_side(temporal.T)
    gram_ref[...] = full(temporal, temporal, (((0,), (0,)), ((), ())))

    def step(g, _):
        at = half * lats + g * many
        guess = times(split(jnp.concatenate([spatial_ref[at + p] for p in range(many)], axis=0)), across)
        coded = jnp.concatenate([coded_ref[g * many + p] for p in range(many)], axis=0)
        put_rows(ref, grid_ref, g, g * many, times(split(jnp.where(coded == GAP, guess, coded)), side))
        return _

    lax.fori_loop(0, spokes // PIECES, step, 0)
    put_block(half, grid_ref, gram_ref, ref)


def last_kernel(sums_ref, days_ref):
    days = days_ref.shape[0]
    days_ref[...] = full(sums_ref[0:days, :], inverse_spd(add_ridge(sums_ref[days:, :])))


SMEM = pl.BlockSpec(memory_space=pltpu.SMEM)
VMEM = pl.BlockSpec(memory_space=pltpu.VMEM)


def call(kernel, outs, specs, scratch, name, flops, nbytes):
    return pl.pallas_call(
        kernel,
        out_shape=[jax.ShapeDtypeStruct(shape, f32) for shape in outs],
        in_specs=specs,
        out_specs=[VMEM] * len(outs),
        scratch_shapes=[pltpu.VMEM(shape, f32) for shape in scratch],
        name=name,
        cost_estimate=pl.CostEstimate(flops=flops, bytes_accessed=nbytes, transcendentals=0),
        compiler_params=pltpu.CompilerParams(vmem_limit_bytes=28 * 1024 * 1024),
    )


def first_call(mine, core, anomaly, observed, seat, days, spokes):
    lats, lons, n = anomaly.shape
    block = (spokes, lats * lons // (2 * spokes) + 16, n)
    grid = (lats // 2, lons, n)
    kernel = functools.partial(first_kernel, mine)
    return call(kernel, [block, grid, grid], [SMEM] + [VMEM] * 4, [grid, (n, n)], "first_projection", 10**9, 10**7)(
        core, anomaly, observed, seat, days
    )


def modes_call(first, core, weight, here, there, days, coded, field):
    lats, lons, n = coded[0].shape
    half = (lats, lons, n)
    grid = (2 * lats, lons, n)
    outs = [grid, (2 * n, n)] + ([half, half] if first else [])
    scratch = [(2 * lats + 2, lons, n), ((8 if first else 4) * lons, n), (4 * n, 2 * n)]
    return call(functools.partial(modes_kernel, first), outs, [SMEM, SMEM] + [VMEM] * 7, scratch, "modes_sweep", 2 * 10**9, 10**7)(
        core, weight, here, there, days, *coded, *field
    )


def days_call(mine, core, sums, coded, spatial, spokes):
    lats, lons, n = coded.shape
    block = (spokes, lats * lons // spokes + 16, n)
    outs = [block] if mine else [block, (sums.shape[0] - n, n)]
    kernel = functools.partial(days_kernel, mine)
    return call(kernel, outs, [SMEM] + [VMEM] * 3, [(lats, lons, n), (n, n)], "days_sweep", 2 * 10**9, 10**7)(
        core, sums, coded, spatial
    )


def last_call(sums):
    n = sums.shape[1]
    return call(last_kernel, [(sums.shape[0] - n, n)], [VMEM], [], "last_days", 10**7, 10**6)(sums)[0]


def lat_weights(first_row, row_count, total_rows):
    index_rows = first_row + jnp.arange(row_count, dtype=jnp.float32)
    angle = (lat_south + lat_span * (index_rows + 0.5) / total_rows) * (math.pi / 180.0)
    cosine = jnp.cos(angle)
    return 1.0 / (cosine * cosine)


def swap_core(value):
    return lax.ppermute(value, "core", [(0, 1), (1, 0)])


def halo_pairs(lats, lons, spokes):
    pairs = []
    for la in range(lats):
        for lo in range(lons):
            for q in range(spokes):
                for core in range(2):
                    if q < spokes // 2:
                        to_la, to_lo = la + 2 * core - 1, lo
                    else:
                        to_la, to_lo = la, lo + (1 if q >= 3 * spokes // 4 else -1)
                    if 0 <= to_la < lats and 0 <= to_lo < lons:
                        here = ((la * lons + lo) * spokes + q) * 2 + core
                        there = ((to_la * lons + to_lo) * spokes + q) * 2 + core
                        pairs.append((here, there))
    return pairs


def gather_all(value, axes, size):
    spread = jnp.broadcast_to(value[None], (size,) + value.shape)
    return lax.all_to_all(spread, axes, 0, 0, tiled=True)


def sum_cells(value):
    size = lax.axis_size("lat") * lax.axis_size("lon")
    rows = value.shape[0]
    parts = lax.all_to_all(value.reshape(size, rows // size, -1), LL, 0, 0, tiled=True)
    mine = jnp.sum(parts, axis=0)
    return gather_all(mine, LL, size).reshape(rows, -1)


def edges_of(grid):
    middle = grid.shape[0] // 2
    up, down = grid[:middle], grid[middle:]
    return jnp.concatenate([up[0], up[:, 0], up[:, -1], down[-1], down[:, 0], down[:, -1]], axis=0)


def on_device(anomaly, observed, ocean_mask, start_days):
    rows_lat, cols_lon, _ = anomaly.shape
    rank_count = start_days.shape[1]
    lats, lons = lax.axis_size("lat"), lax.axis_size("lon")
    spokes = lax.axis_size("zlo") * lax.axis_size("y")
    core = lax.axis_index("core")
    spoke = lax.axis_index("zlo") * lax.axis_size("y") + lax.axis_index("y")
    pairs = halo_pairs(lats, lons, spokes)
    cells = rows_lat * cols_lon // (2 * spokes)
    core_word = core.reshape(1, 1).astype(jnp.int32)
    sea_grid = ocean_mask.astype(f32)
    seat = jnp.pad(sea_grid.T, ((0, 0), (0, rank_count - rows_lat)))
    first_lat = (lax.axis_index("lat") * rows_lat).astype(f32)
    weight = lat_weights(first_lat, rows_lat, float(rows_lat * lats)).reshape(1, rows_lat)
    edge_sea = lax.dynamic_slice_in_dim(edges_of(sea_grid), (core * spokes + spoke) * 8, 8)
    edge_sea = jnp.broadcast_to(edge_sea[:, None], (8, rank_count))
    temporal = start_days
    coded, field = [None, None], [None, None]
    other, coded[1], field[1] = first_call(False, core_word, anomaly, observed, seat, start_days, spokes)
    mine, coded[0], field[0] = first_call(True, core_word, anomaly, observed, seat, start_days, spokes)
    for sweep in range(ITERS):
        half = mine + swap_core(other)
        shard = jnp.sum(lax.all_to_all(half, YZ, 0, 0, tiled=True), axis=0)
        send = shard[cells : cells + 8]
        if sweep == 0:
            send = jnp.concatenate([send, edge_sea], axis=0)
        halo = lax.ppermute(send, ALL, pairs)
        shard = jnp.concatenate([shard[:cells], halo, shard[cells + 8 :]], axis=0)
        here = gather_all(shard, YZ, spokes)
        there = swap_core(here)
        out = modes_call(sweep == 0, core_word, weight, here, there, temporal, coded, field)
        spatial, sums = out[0], sum_cells(out[1])
        if sweep == 0:
            field = out[2:4]
        if sweep < ITERS - 1:
            other, temporal = days_call(False, core_word, sums, coded[1], spatial, spokes)
            (mine,) = days_call(True, core_word, temporal, coded[0], spatial, spokes)
        else:
            temporal = last_call(sums)
    return (spatial, temporal)


def solution(mesh):
    lats, lons, days = mesh.devices.shape
    fine = Mesh(mesh.devices.reshape(lats, lons, 2, days // 4, 2), ALL)
    in_specs = (P("lat", "lon", DAY), P("lat", "lon", DAY), P("lat", "lon"), P(DAY, None))
    out_specs = (P("lat", "lon", None), P(DAY, None))
    return jax.shard_map(
        on_device, mesh=fine, in_specs=in_specs, out_specs=out_specs, check_vma=False
    )
```

```python
import functools
import math

import jax
import jax.numpy as jnp
from jax import lax
from jax.experimental import pallas as pl
from jax.experimental.pallas import tpu as pltpu
from jax.sharding import Mesh, PartitionSpec as P

ITERS = 2


ridge_term = 1.0
diffusion = 0.1
lat_south = 30.0
lat_span = 16.0

GAP = 1e30
PIECES = 8
GROUP = 16
ROOM = 58
YZ = ("zlo", "y")
DAY = ("zlo", "y", "core")
ALL = ("lat", "lon", "zlo", "y", "core")
LL = ("lat", "lon")
f32, bf16 = jnp.float32, jnp.bfloat16


def inverse_spd(matrix):
    size = matrix.shape[0]
    blocks = [matrix[8 * r : 8 * r + 8] for r in range(size // 8)]
    lane = lax.broadcasted_iota(jnp.int32, (1, size), 1)
    row = lax.broadcasted_iota(jnp.int32, (8, size), 0)
    for k in range(0, size, 4):
        home, off = k // 8, k % 8
        rows = [blocks[home][off + i : off + i + 1] for i in range(4)]
        d = [[jnp.broadcast_to(rows[i][:, k + j : k + j + 1], (1, size)) for j in range(4)] for i in range(4)]
        in_panel = (lane >= k) & (lane < k + 4)
        a, b, c = d[0][0], d[0][1], d[1][1]
        r = 1.0 / (a * c - b * b)
        a00, a01, a11 = c * r, -b * r, a * r
        b02, b03, b12, b13 = d[0][2], d[0][3], d[1][2], d[1][3]
        g02, g03 = a00 * b02 + a01 * b12, a00 * b03 + a01 * b13
        g12, g13 = a01 * b02 + a11 * b12, a01 * b03 + a11 * b13
        s22 = d[2][2] - (b02 * g02 + b12 * g12)
        s23 = d[2][3] - (b02 * g03 + b12 * g13)
        s33 = d[3][3] - (b03 * g03 + b13 * g13)
        r = 1.0 / (s22 * s33 - s23 * s23)
        i22, i23, i33 = s33 * r, -s23 * r, s22 * r
        h02, h03 = g02 * i22 + g03 * i23, g02 * i23 + g03 * i33
        h12, h13 = g12 * i22 + g13 * i23, g12 * i23 + g13 * i33
        q00 = a00 + (h02 * g02 + h03 * g03)
        q01 = a01 + (h02 * g12 + h03 * g13)
        q11 = a11 + (h12 * g12 + h13 * g13)
        inv = [[q00, q01, -h02, -h03], [q01, q11, -h12, -h13], [-h02, -h12, i22, i23], [-h03, -h13, i23, i33]]
        unit = [jnp.where(lane == k + j, 1.0, jnp.where(in_panel, 0.0, rows[j])) for j in range(4)]
        new = [
            (inv[i][0] * unit[0] + inv[i][1] * unit[1]) + (inv[i][2] * unit[2] + inv[i][3] * unit[3])
            for i in range(4)
        ]
        out = []
        for r8, block in enumerate(blocks):
            cols = [block[:, k + j : k + j + 1] for j in range(4)]
            keep = jnp.where(in_panel, 0.0, block)
            keep = keep - ((cols[0] * new[0] + cols[1] * new[1]) + (cols[2] * new[2] + cols[3] * new[3]))
            if r8 == home:
                for j in range(4):
                    keep = jnp.where(row == off + j, new[j], keep)
            out.append(keep)
        blocks = out
    return jnp.concatenate(blocks, axis=0)


def add_ridge(gram):
    size = gram.shape[0]
    same = lax.broadcasted_iota(jnp.int32, (size, size), 0) == lax.broadcasted_iota(jnp.int32, (size, size), 1)
    return gram + jnp.where(same, ridge_term, 0.0)


def split(value):
    one = value.astype(bf16)
    return jnp.concatenate([one, (value - one.astype(f32)).astype(bf16)], axis=1)


def right_side(value):
    wide = split(value)
    return jnp.concatenate([wide, wide], axis=0)


def times(parts, side):
    wide = jnp.dot(parts, side, preferred_element_type=f32)
    n = wide.shape[1] // 2
    return wide[:, :n] + wide[:, n:]


def dot_tn(left, right):
    return lax.dot_general(left, right, (((0,), (0,)), ((), ())), preferred_element_type=f32)


def full(left, right, dims=(((1,), (0,)), ((), ()))):
    return lax.dot_general(left, right, dims, precision=lax.Precision.HIGHEST, preferred_element_type=f32)


def put_block(half, grid_ref, gram_ref, ref):
    lats, lons, modes = grid_ref.shape
    spokes = ref.shape[0]
    cells = lats * lons // spokes
    line = grid_ref[half * (lats - 1)]
    for q in range(spokes):
        if q < lons // 8:
            edge = line[8 * q : 8 * q + 8]
        else:
            side, at = divmod(8 * q - lons, lats)
            edge = grid_ref[at : at + 8, side * (lons - 1), :]
        ref[q, cells : cells + 8, :] = edge
        ref[q, cells + 8 : cells + 16, :] = gram_ref[8 * q : 8 * q + 8, :]


def put_rows(ref, grid_ref, g, base, out):
    lons = grid_ref.shape[1]
    cells = ref.shape[1] - 16
    for p in range(PIECES):
        ref[g * PIECES + p, 0:cells, :] = out[p * cells : (p + 1) * cells]
    for p in range(out.shape[0] // lons):
        grid_ref[base + p] = out[p * lons : (p + 1) * lons]


def fetch(pairs, sems):
    copies = [pltpu.make_async_copy(src, dst, sems.at[n]) for n, (src, dst) in enumerate(pairs)]
    for copy in copies:
        copy.start()
    return copies


def first_kernel(
    mine, core_ref, anomaly_hbm, observed_hbm, mask_hbm, days_hbm, ref, coded_hbm, sea_hbm,
    grid_ref, gram_ref, anomaly_ref, observed_ref, mask_ref, days_ref, coded_ref, sea_ref, sems,
):
    core = core_ref[0, 0]
    half = core if mine else 1 - core
    lats, lons, days = coded_ref.shape
    spokes = ref.shape[0]
    many = PIECES * lats // spokes
    part = pl.ds(half * lats, lats)
    copies = fetch(
        [
            (days_hbm, days_ref),
            (mask_hbm, mask_ref),
            (anomaly_hbm.at[part], anomaly_ref),
            (observed_hbm.at[part], observed_ref),
        ],
        sems,
    )
    copies[0].wait()
    temporal = days_ref[...]
    side = right_side(temporal)
    gram_ref[...] = full(temporal, temporal, (((0,), (0,)), ((), ())))
    copies[1].wait()
    mask = mask_ref[...].astype(f32)
    seat = jnp.concatenate([mask, jnp.zeros((days - mask.shape[0], lons), f32)], axis=0).T
    copies[2].wait()
    copies[3].wait()

    def step(g, _):
        rows = []
        for p in range(many):
            here = g * many + p
            i = half * lats + here
            sea = jnp.broadcast_to(pltpu.roll(seat, lax.rem(seat.shape[1] - i, seat.shape[1]), 1)[:, :1], (lons, days))
            sea_ref[here] = sea
            seen = observed_ref[here] != 0
            known = jnp.where(seen, sea * anomaly_ref[here], 0.0)
            coded_ref[here] = jnp.where(seen | (sea == 0.0), known, GAP)
            rows.append(known)
        put_rows(ref, grid_ref, g, g * many, times(split(jnp.concatenate(rows, axis=0)), side))
        return _

    lax.fori_loop(0, spokes // PIECES, step, 0)
    copies = fetch([(coded_ref, coded_hbm), (sea_ref, sea_hbm)], sems)
    put_block(half, grid_ref, gram_ref, ref)
    for copy in copies:
        copy.wait()


def modes_kernel(first, core_ref, weight_ref, here_hbm, there_hbm, days_ref, *refs):
    coded_hbm, field_hbm, refs = refs[0:2], refs[2:4], refs[4:]
    spatial_hbm, sums_ref = refs[0:2]
    around_hbm, refs = refs[2 : (4 if first else 2)], refs[(4 if first else 2) :]
    pad_ref, rim_ref, wide_ref, spatial_ref = refs[0:4]
    coded_refs, field_refs, refs = refs[4:6], refs[6:8], refs[8:]
    around_refs = refs[0:2] if first else field_refs
    gram_ref, here_ref, there_ref, in_sems, out_sems = refs[-5:]
    core = core_ref[0, 0]
    lats, lons, modes = spatial_ref.shape
    deep = lats // 2
    spokes = here_ref.shape[0]
    per = deep // spokes
    cells = per * lons
    tiles = 2 if first else 1
    gram_at = cells + 8 * tiles
    halves = (core, 1 - core)
    loads = fetch(
        [(here_hbm.at[:, pl.ds(gram_at, 8)], gram_ref), (here_hbm, here_ref), (there_hbm, there_ref)]
        + list(zip((*field_hbm, *coded_hbm), (*field_refs, *coded_refs))),
        in_sems,
    )
    loads[0].wait()
    inverse_side = right_side(inverse_spd(add_ridge(gram_ref[...].reshape(modes, modes))))
    days_side = right_side(days_ref[...].T)
    for copy in loads[1:]:
        copy.wait()
    stores = []

    for half, ref in zip(halves, (here_ref, there_ref)):
        for q in range(spokes):
            for p in range(per):
                pad_ref[half * deep + q * per + p + 1] = ref[q, p * lons : (p + 1) * lons, :]
            if q < lons // 8:
                at = half * lons + 8 * q
            else:
                side, along = divmod(8 * q - lons, deep)
                at = 2 * lons + side * lats + half * deep + along
            for t in range(tiles):
                rim_ref[pl.ds(pl.multiple_of(t * 4 * lons + at, 8), 8), :] = ref[q, cells + 8 * t : cells + 8 * t + 8, :]
    pad_ref[0] = rim_ref[lons : 2 * lons, :]
    pad_ref[lats + 1] = rim_ref[0:lons, :]
    row = lax.broadcasted_iota(jnp.int32, (lons, modes), 0)

    def beside(value, i, kind):
        east = rim_ref[pl.ds(kind * 4 * lons + 2 * lons + i, 1), :]
        west = rim_ref[pl.ds(kind * 4 * lons + 2 * lons + lats + i, 1), :]
        ahead = jnp.where(row == lons - 1, east, pltpu.roll(value, lons - 1, 0))
        behind = jnp.where(row == 0, west, pltpu.roll(value, 1, 0))
        return ahead + behind

    if first:
        for n, half in enumerate(halves):
            field_ref, beyond_ref, around_ref = field_refs[n], field_refs[1 - n], around_refs[n]

            def masks(l, _, half=half, field_ref=field_ref, beyond_ref=beyond_ref, around_ref=around_ref):
                i = half * deep + l
                sea = field_ref[l]
                above = jnp.where(half == 0, rim_ref[5 * lons : 6 * lons, :], beyond_ref[deep - 1])
                below = jnp.where(half == 0, beyond_ref[0], rim_ref[4 * lons : 5 * lons, :])
                north = jnp.where(l == 0, above, field_ref[jnp.maximum(l - 1, 0)])
                south = jnp.where(l == deep - 1, below, field_ref[jnp.minimum(l + 1, deep - 1)])
                round_ = (north + south) + weight_ref[0, i] * beside(sea, i, 1)
                around_ref[l] = jnp.where(sea == 0.0, GAP, 1.0 - diffusion * round_)
                return _

            lax.fori_loop(0, deep, masks, 0, unroll=2)
            stores += fetch([(around_ref, around_hbm[n])], out_sems.at[pl.ds(2 + n, 1)])

    wide_ref[...] = jnp.zeros_like(wide_ref)
    for n, half in enumerate(halves):

        def step(g, _, half=half, around_ref=around_refs[n], coded_ref=coded_refs[n]):
            smoothed = []
            for p in range(GROUP):
                l = g * GROUP + p
                i = half * deep + l
                around = around_ref[l]
                raw = pad_ref[i + 1]
                near = (pad_ref[i] + pad_ref[i + 2]) + weight_ref[0, i] * beside(raw, i, 0)
                smoothed.append(jnp.where(around == GAP, 0.0, around * raw + diffusion * near))
            spatial = times(split(jnp.concatenate(smoothed, axis=0)), inverse_side)
            parts = split(spatial)
            guess = times(parts, days_side)
            filled = []
            for p in range(GROUP):
                l = g * GROUP + p
                spatial_ref[half * deep + l] = spatial[p * lons : (p + 1) * lons]
                coded = coded_ref[l]
                filled.append(jnp.where(coded == GAP, guess[p * lons : (p + 1) * lons], coded))
            filled = split(jnp.concatenate(filled, axis=0))
            wide_ref[...] += dot_tn(jnp.concatenate([filled, parts], axis=1), parts)
            return _

        lax.fori_loop(0, deep // GROUP, step, 0)
        part = pl.ds(half * deep, deep)
        stores += fetch([(spatial_ref.at[part], spatial_hbm.at[part])], out_sems.at[pl.ds(n, 1)])
    m = modes
    for part in range(2):
        at = 2 * part * m
        wide = wide_ref[at : at + m, :] + wide_ref[at + m : at + 2 * m, :]
        sums_ref[part * m : (part + 1) * m, :] = wide[:, :m] + wide[:, m:]
    for copy in stores:
        copy.wait()


def days_kernel(mine, core_ref, sums_ref, coded_hbm, spatial_hbm, ref, *refs):
    core = core_ref[0, 0]
    half = core if mine else 1 - core
    grid_ref, gram_ref, coded_ref, spatial_ref, sems = refs[-5:]
    lats, lons, modes = coded_ref.shape
    loads = fetch([(coded_hbm, coded_ref), (spatial_hbm.at[pl.ds(half * lats, lats)], spatial_ref)], sems)
    spokes = ref.shape[0]
    many = PIECES * lats // spokes
    if mine:
        temporal = sums_ref[...]
    else:
        days = sums_ref.shape[0] - modes
        temporal = full(sums_ref[0:days, :], inverse_spd(add_ridge(sums_ref[days:, :])))
        refs[0][...] = temporal
    side = right_side(temporal)
    across = right_side(temporal.T)
    gram_ref[...] = full(temporal, temporal, (((0,), (0,)), ((), ())))

    for copy in loads:
        copy.wait()

    def step(g, _):
        at = g * many
        guess = times(split(jnp.concatenate([spatial_ref[at + p] for p in range(many)], axis=0)), across)
        coded = jnp.concatenate([coded_ref[g * many + p] for p in range(many)], axis=0)
        put_rows(ref, grid_ref, g, g * many, times(split(jnp.where(coded == GAP, guess, coded)), side))
        return _

    lax.fori_loop(0, spokes // PIECES, step, 0)
    put_block(half, grid_ref, gram_ref, ref)


def last_kernel(sums_ref, days_ref):
    days = days_ref.shape[0]
    days_ref[...] = full(sums_ref[0:days, :], inverse_spd(add_ridge(sums_ref[days:, :])))


SMEM = pl.BlockSpec(memory_space=pltpu.SMEM)
VMEM = pl.BlockSpec(memory_space=pltpu.VMEM)
HBM = pl.BlockSpec(memory_space=pltpu.HBM)


def call(kernel, outs, specs, scratch, name, flops, nbytes, room=60):
    return pl.pallas_call(
        kernel,
        out_shape=[jax.ShapeDtypeStruct(shape, f32) for shape, _ in outs],
        in_specs=specs,
        out_specs=[place for _, place in outs],
        scratch_shapes=[pltpu.VMEM(shape, f32) if isinstance(shape, tuple) else shape for shape in scratch],
        name=name,
        cost_estimate=pl.CostEstimate(flops=flops, bytes_accessed=nbytes, transcendentals=0),
        compiler_params=pltpu.CompilerParams(vmem_limit_bytes=room * 1024 * 1024),
    )


def copy_sems(count):
    return pltpu.SemaphoreType.DMA((count,))


def first_call(mine, core, anomaly, observed, mask, days, spokes):
    lats, lons, n = anomaly.shape
    block = (spokes, lats * lons // (2 * spokes) + 16, n)
    grid = (lats // 2, lons, n)
    scratch = [grid, (n, n), grid, pltpu.VMEM(grid, jnp.int32), pltpu.VMEM(mask.shape, jnp.int32), (n, n), grid, grid, copy_sems(4)]
    outs = [(block, VMEM), (grid, HBM), (grid, HBM)]
    return call(functools.partial(first_kernel, mine), outs, [SMEM] + [HBM] * 4, scratch, "first_projection", 10**9, 10**7)(
        core, anomaly, observed, mask, days
    )


def modes_call(first, core, weight, here, there, days, coded, field):
    lats, lons, n = coded[0].shape
    half = (lats, lons, n)
    grid = (2 * lats, lons, n)
    outs = [(grid, HBM), ((2 * n, n), VMEM)] + ([(half, HBM)] * 2 if first else [])
    scratch = [(2 * lats + 2, lons, n), ((8 if first else 4) * lons, n), (4 * n, 2 * n), grid] + [half] * (6 if first else 4)
    scratch += [(here.shape[0], 8, n), here.shape, here.shape, copy_sems(7), copy_sems(4)]
    specs = [SMEM, SMEM, HBM, HBM, VMEM] + [HBM] * 4
    return call(functools.partial(modes_kernel, first), outs, specs, scratch, "modes_sweep", 2 * 10**9, 10**7, ROOM)(
        core, weight, here, there, days, *coded, *field
    )


def days_call(mine, core, sums, coded, spatial, spokes):
    lats, lons, n = coded.shape
    block = (spokes, lats * lons // spokes + 16, n)
    outs = [(block, VMEM)] if mine else [(block, VMEM), ((sums.shape[0] - n, n), VMEM)]
    grid = (lats, lons, n)
    scratch = [grid, (n, n), grid, grid, copy_sems(2)]
    return call(functools.partial(days_kernel, mine), outs, [SMEM, VMEM, HBM, HBM], scratch, "days_sweep", 2 * 10**9, 10**7)(
        core, sums, coded, spatial
    )


def last_call(sums):
    n = sums.shape[1]
    return call(last_kernel, [((sums.shape[0] - n, n), VMEM)], [VMEM], [], "last_days", 10**7, 10**6, 16)(sums)[0]


def lat_weights(first_row, row_count, total_rows):
    index_rows = first_row + jnp.arange(row_count, dtype=jnp.float32)
    angle = (lat_south + lat_span * (index_rows + 0.5) / total_rows) * (math.pi / 180.0)
    cosine = jnp.cos(angle)
    return 1.0 / (cosine * cosine)


def swap_core(value):
    return lax.ppermute(value, "core", [(0, 1), (1, 0)])


def halo_pairs(lats, lons, spokes):
    pairs = []
    for la in range(lats):
        for lo in range(lons):
            for q in range(spokes):
                for core in range(2):
                    if q < spokes // 2:
                        to_la, to_lo = la + 2 * core - 1, lo
                    else:
                        to_la, to_lo = la, lo + (1 if q >= 3 * spokes // 4 else -1)
                    if 0 <= to_la < lats and 0 <= to_lo < lons:
                        here = ((la * lons + lo) * spokes + q) * 2 + core
                        there = ((to_la * lons + to_lo) * spokes + q) * 2 + core
                        pairs.append((here, there))
    return pairs


def gather_all(value, axes, size):
    spread = jnp.broadcast_to(value[None], (size,) + value.shape)
    return lax.all_to_all(spread, axes, 0, 0, tiled=True)


def sum_cells(value):
    size = lax.axis_size("lat") * lax.axis_size("lon")
    rows = value.shape[0]
    parts = lax.all_to_all(value.reshape(size, rows // size, -1), LL, 0, 0, tiled=True)
    mine = jnp.sum(parts, axis=0)
    return gather_all(mine, LL, size).reshape(rows, -1)


def edges_of(grid):
    middle = grid.shape[0] // 2
    up, down = grid[:middle], grid[middle:]
    return jnp.concatenate([up[0], up[:, 0], up[:, -1], down[-1], down[:, 0], down[:, -1]], axis=0)


def on_device(anomaly, observed, ocean_mask, start_days):
    rows_lat, cols_lon, _ = anomaly.shape
    rank_count = start_days.shape[1]
    lats, lons = lax.axis_size("lat"), lax.axis_size("lon")
    spokes = lax.axis_size("zlo") * lax.axis_size("y")
    core = lax.axis_index("core")
    spoke = lax.axis_index("zlo") * lax.axis_size("y") + lax.axis_index("y")
    pairs = halo_pairs(lats, lons, spokes)
    cells = rows_lat * cols_lon // (2 * spokes)
    core_word = core.reshape(1, 1).astype(jnp.int32)
    sea_grid = ocean_mask.astype(f32)
    first_lat = (lax.axis_index("lat") * rows_lat).astype(f32)
    weight = lat_weights(first_lat, rows_lat, float(rows_lat * lats)).reshape(1, rows_lat)
    edge_sea = lax.dynamic_slice_in_dim(edges_of(sea_grid), (core * spokes + spoke) * 8, 8)
    edge_sea = jnp.broadcast_to(edge_sea[:, None], (8, rank_count))
    temporal = start_days
    coded, field = [None, None], [None, None]
    other, coded[1], field[1] = first_call(False, core_word, anomaly, observed, ocean_mask, start_days, spokes)
    mine, coded[0], field[0] = first_call(True, core_word, anomaly, observed, ocean_mask, start_days, spokes)
    for sweep in range(ITERS):
        half = mine + swap_core(other)
        shard = jnp.sum(lax.all_to_all(half, YZ, 0, 0, tiled=True), axis=0)
        send = shard[cells : cells + 8]
        if sweep == 0:
            send = jnp.concatenate([send, edge_sea], axis=0)
        halo = lax.ppermute(send, ALL, pairs)
        shard = jnp.concatenate([shard[:cells], halo, shard[cells + 8 :]], axis=0)
        here = gather_all(shard, YZ, spokes)
        there = swap_core(here)
        out = modes_call(sweep == 0, core_word, weight, here, there, temporal, coded, field)
        spatial, sums = out[0], sum_cells(out[1])
        if sweep == 0:
            field = out[2:4]
        if sweep < ITERS - 1:
            other, temporal = days_call(False, core_word, sums, coded[1], spatial, spokes)
            (mine,) = days_call(True, core_word, temporal, coded[0], spatial, spokes)
        else:
            temporal = last_call(sums)
    return (spatial, temporal)


def solution(mesh):
    lats, lons, days = mesh.devices.shape
    fine = Mesh(mesh.devices.reshape(lats, lons, 2, days // 4, 2), ALL)
    in_specs = (P("lat", "lon", DAY), P("lat", "lon", DAY), P("lat", "lon"), P(DAY, None))
    out_specs = (P("lat", "lon", None), P(DAY, None))
    return jax.shard_map(
        on_device, mesh=fine, in_specs=in_specs, out_specs=out_specs, check_vma=False
    )
```

```python
import functools
import math

import jax
import jax.numpy as jnp
from jax import lax
from jax.experimental import pallas as pl
from jax.experimental.pallas import tpu as pltpu
from jax.sharding import Mesh, PartitionSpec as P

ITERS = 2


ridge_term = 1.0
diffusion = 0.1
lat_south = 30.0
lat_span = 16.0

GAP = 1e30
PIECES = 8
GROUP = 16
FIRST_ROOM = 57
ROOM = 50
SHELF = 384
YZ = ("zlo", "y")
DAY = ("zlo", "y", "core")
ALL = ("lat", "lon", "zlo", "y", "core")
LL = ("lat", "lon")
f32, bf16 = jnp.float32, jnp.bfloat16


def inverse_spd(matrix):
    size = matrix.shape[0]
    blocks = [matrix[8 * r : 8 * r + 8] for r in range(size // 8)]
    lane = lax.broadcasted_iota(jnp.int32, (1, size), 1)
    row = lax.broadcasted_iota(jnp.int32, (8, size), 0)
    for k in range(0, size, 4):
        home, off = k // 8, k % 8
        rows = [blocks[home][off + i : off + i + 1] for i in range(4)]
        d = [[jnp.broadcast_to(rows[i][:, k + j : k + j + 1], (1, size)) for j in range(4)] for i in range(4)]
        in_panel = (lane >= k) & (lane < k + 4)
        a, b, c = d[0][0], d[0][1], d[1][1]
        r = 1.0 / (a * c - b * b)
        a00, a01, a11 = c * r, -b * r, a * r
        b02, b03, b12, b13 = d[0][2], d[0][3], d[1][2], d[1][3]
        g02, g03 = a00 * b02 + a01 * b12, a00 * b03 + a01 * b13
        g12, g13 = a01 * b02 + a11 * b12, a01 * b03 + a11 * b13
        s22 = d[2][2] - (b02 * g02 + b12 * g12)
        s23 = d[2][3] - (b02 * g03 + b12 * g13)
        s33 = d[3][3] - (b03 * g03 + b13 * g13)
        r = 1.0 / (s22 * s33 - s23 * s23)
        i22, i23, i33 = s33 * r, -s23 * r, s22 * r
        h02, h03 = g02 * i22 + g03 * i23, g02 * i23 + g03 * i33
        h12, h13 = g12 * i22 + g13 * i23, g12 * i23 + g13 * i33
        q00 = a00 + (h02 * g02 + h03 * g03)
        q01 = a01 + (h02 * g12 + h03 * g13)
        q11 = a11 + (h12 * g12 + h13 * g13)
        inv = [[q00, q01, -h02, -h03], [q01, q11, -h12, -h13], [-h02, -h12, i22, i23], [-h03, -h13, i23, i33]]
        unit = [jnp.where(lane == k + j, 1.0, jnp.where(in_panel, 0.0, rows[j])) for j in range(4)]
        new = [
            (inv[i][0] * unit[0] + inv[i][1] * unit[1]) + (inv[i][2] * unit[2] + inv[i][3] * unit[3])
            for i in range(4)
        ]
        out = []
        for r8, block in enumerate(blocks):
            cols = [block[:, k + j : k + j + 1] for j in range(4)]
            keep = jnp.where(in_panel, 0.0, block)
            keep = keep - ((cols[0] * new[0] + cols[1] * new[1]) + (cols[2] * new[2] + cols[3] * new[3]))
            if r8 == home:
                for j in range(4):
                    keep = jnp.where(row == off + j, new[j], keep)
            out.append(keep)
        blocks = out
    return jnp.concatenate(blocks, axis=0)


def add_ridge(gram):
    size = gram.shape[0]
    same = lax.broadcasted_iota(jnp.int32, (size, size), 0) == lax.broadcasted_iota(jnp.int32, (size, size), 1)
    return gram + jnp.where(same, ridge_term, 0.0)


def split(value):
    one = value.astype(bf16)
    return jnp.concatenate([one, (value - one.astype(f32)).astype(bf16)], axis=1)


def right_side(value):
    wide = split(value)
    return jnp.concatenate([wide, wide], axis=0)


def times(parts, side):
    wide = jnp.dot(parts, side, preferred_element_type=f32)
    n = wide.shape[1] // 2
    return wide[:, :n] + wide[:, n:]


def dot_tn(left, right):
    return lax.dot_general(left, right, (((0,), (0,)), ((), ())), preferred_element_type=f32)


def full(left, right, dims=(((1,), (0,)), ((), ()))):
    return lax.dot_general(left, right, dims, precision=lax.Precision.HIGHEST, preferred_element_type=f32)


def put_block(half, grid_ref, gram_ref, ref):
    lats, lons, modes = grid_ref.shape
    spokes = ref.shape[0]
    cells = lats * lons // spokes
    line = grid_ref[half * (lats - 1)]
    for q in range(spokes):
        if q < lons // 8:
            edge = line[8 * q : 8 * q + 8]
        else:
            side, at = divmod(8 * q - lons, lats)
            edge = grid_ref[at : at + 8, side * (lons - 1), :]
        ref[q, cells : cells + 8, :] = edge
        ref[q, cells + 8 : cells + 16, :] = gram_ref[8 * q : 8 * q + 8, :]


def put_rows(ref, grid_ref, g, base, out):
    lons = grid_ref.shape[1]
    cells = ref.shape[1] - 16
    for p in range(PIECES):
        ref[g * PIECES + p, 0:cells, :] = out[p * cells : (p + 1) * cells]
    for p in range(out.shape[0] // lons):
        grid_ref[base + p] = out[p * lons : (p + 1) * lons]


def fetch(pairs, sems):
    copies = [pltpu.make_async_copy(src, dst, sems.at[n]) for n, (src, dst) in enumerate(pairs)]
    for copy in copies:
        copy.start()
    return copies


def first_kernel(
    mine, core_ref, anomaly_hbm, observed_hbm, mask_hbm, days_hbm, ref, shelf_hbm,
    grid_ref, gram_ref, anomaly_ref, observed_ref, mask_ref, days_ref, coded_ref, sea_ref, seat_ref, sems,
):
    core = core_ref[0, 0]
    half = core if mine else 1 - core
    lats, lons, days = coded_ref.shape
    spokes = ref.shape[0]
    many = PIECES * lats // spokes
    groups = spokes // PIECES
    small = fetch([(days_hbm, days_ref), (mask_hbm, mask_ref)], sems)
    loads, stores = [], []
    for g in range(groups):
        away, near = pl.ds(half * lats + g * many, many), pl.ds(g * many, many)
        pairs = [(anomaly_hbm.at[away], anomaly_ref.at[near]), (observed_hbm.at[away], observed_ref.at[near])]
        loads.append(fetch(pairs, sems.at[pl.ds(2 + 2 * g, 2)]))
    small[0].wait()
    temporal = days_ref[...]
    side = right_side(temporal)
    gram_ref[...] = full(temporal, temporal, (((0,), (0,)), ((), ())))
    small[1].wait()
    mask = mask_ref[...].astype(f32)
    seat_ref[...] = jnp.concatenate([mask, jnp.zeros((days - mask.shape[0], lons), f32)], axis=0).T
    for g in range(groups):
        for copy in loads[g]:
            copy.wait()

        def step(_, carry, g=g):
            rows = []
            for p in range(many):
                here = g * many + p
                i = half * lats + here
                turned = pltpu.roll(seat_ref[...], lax.rem(days - i, days), 1)
                sea = jnp.broadcast_to(turned[:, :1], (lons, days))
                sea_ref[here] = sea
                seen = observed_ref[here] != 0
                known = jnp.where(seen, sea * anomaly_ref[here], 0.0)
                coded_ref[here] = jnp.where(seen | (sea == 0.0), known, GAP)
                rows.append(known)
            put_rows(ref, grid_ref, g, g * many, times(split(jnp.concatenate(rows, axis=0)), side))
            return carry

        step(0, 0)
        near = pl.ds(g * many, many)
        pairs = [(coded_ref.at[near], shelf_hbm.at[near]), (sea_ref.at[near], shelf_hbm.at[pl.ds(lats + g * many, many)])]
        stores += fetch(pairs, sems.at[pl.ds(2 + 2 * groups + 2 * g, 2)])
    put_block(half, grid_ref, gram_ref, ref)
    for copy in stores:
        copy.wait()


def modes_kernel(first, core_ref, weight_ref, here_ref, there_ref, days_ref, *refs):
    shelves, refs = refs[0 : (2 if first else 3)], refs[(2 if first else 3) :]
    out_hbm, sums_ref, pad_ref, rim_ref, wide_ref, spatial_ref = refs[0:6]
    coded_refs, field_refs, refs = refs[6:8], refs[8:10], refs[10:]
    around_refs = refs[0:2] if first else field_refs
    in_sems, out_sems = refs[-2:]
    core = core_ref[0, 0]
    lats, lons, modes = spatial_ref.shape
    deep = lats // 2
    spokes = here_ref.shape[0]
    per = deep // spokes
    cells = per * lons
    tiles = 2 if first else 1
    gram_at = cells + 8 * tiles
    halves = (core, 1 - core)
    fields = [(shelves[n], deep) if first else (shelves[2], n * deep) for n in range(2)]
    pairs = [(shelf.at[pl.ds(at, deep)], field_refs[n]) for n, (shelf, at) in enumerate(fields)]
    pairs += [(shelves[n].at[pl.ds(0, deep)], coded_refs[n]) for n in range(2)]
    loads = fetch(pairs, in_sems)
    gram = jnp.concatenate([here_ref[q, gram_at : gram_at + 8, :] for q in range(spokes)], axis=0)
    inverse_side = right_side(inverse_spd(add_ridge(gram)))
    days_side = right_side(days_ref[...].T)
    for copy in loads:
        copy.wait()
    stores = []

    for half, ref in zip(halves, (here_ref, there_ref)):
        for q in range(spokes):
            for p in range(per):
                pad_ref[half * deep + q * per + p + 1] = ref[q, p * lons : (p + 1) * lons, :]
            if q < lons // 8:
                at = half * lons + 8 * q
            else:
                side, along = divmod(8 * q - lons, deep)
                at = 2 * lons + side * lats + half * deep + along
            for t in range(tiles):
                rim_ref[pl.ds(pl.multiple_of(t * 4 * lons + at, 8), 8), :] = ref[q, cells + 8 * t : cells + 8 * t + 8, :]
    pad_ref[0] = rim_ref[lons : 2 * lons, :]
    pad_ref[lats + 1] = rim_ref[0:lons, :]
    row = lax.broadcasted_iota(jnp.int32, (lons, modes), 0)

    def beside(value, i, kind):
        east = rim_ref[pl.ds(kind * 4 * lons + 2 * lons + i, 1), :]
        west = rim_ref[pl.ds(kind * 4 * lons + 2 * lons + lats + i, 1), :]
        ahead = jnp.where(row == lons - 1, east, pltpu.roll(value, lons - 1, 0))
        behind = jnp.where(row == 0, west, pltpu.roll(value, 1, 0))
        return ahead + behind

    if first:
        for n, half in enumerate(halves):
            field_ref, beyond_ref, around_ref = field_refs[n], field_refs[1 - n], around_refs[n]

            def masks(l, _, half=half, field_ref=field_ref, beyond_ref=beyond_ref, around_ref=around_ref):
                i = half * deep + l
                sea = field_ref[l]
                above = jnp.where(half == 0, rim_ref[5 * lons : 6 * lons, :], beyond_ref[deep - 1])
                below = jnp.where(half == 0, beyond_ref[0], rim_ref[4 * lons : 5 * lons, :])
                north = jnp.where(l == 0, above, field_ref[jnp.maximum(l - 1, 0)])
                south = jnp.where(l == deep - 1, below, field_ref[jnp.minimum(l + 1, deep - 1)])
                round_ = (north + south) + weight_ref[0, i] * beside(sea, i, 1)
                around_ref[l] = jnp.where(sea == 0.0, GAP, 1.0 - diffusion * round_)
                return _

            lax.fori_loop(0, deep, masks, 0, unroll=2)
            stores += fetch([(around_ref, out_hbm.at[pl.ds(n * deep, deep)])], out_sems.at[pl.ds(2 + n, 1)])

    wide_ref[...] = jnp.zeros_like(wide_ref)
    for n, half in enumerate(halves):

        def step(g, _, half=half, around_ref=around_refs[n], coded_ref=coded_refs[n]):
            smoothed = []
            for p in range(GROUP):
                l = g * GROUP + p
                i = half * deep + l
                around = around_ref[l]
                raw = pad_ref[i + 1]
                near = (pad_ref[i] + pad_ref[i + 2]) + weight_ref[0, i] * beside(raw, i, 0)
                smoothed.append(jnp.where(around == GAP, 0.0, around * raw + diffusion * near))
            spatial = times(split(jnp.concatenate(smoothed, axis=0)), inverse_side)
            parts = split(spatial)
            guess = times(parts, days_side)
            filled = []
            for p in range(GROUP):
                l = g * GROUP + p
                spatial_ref[half * deep + l] = spatial[p * lons : (p + 1) * lons]
                coded = coded_ref[l]
                filled.append(jnp.where(coded == GAP, guess[p * lons : (p + 1) * lons], coded))
            filled = split(jnp.concatenate(filled, axis=0))
            wide_ref[...] += dot_tn(jnp.concatenate([filled, parts], axis=1), parts)
            return _

        lax.fori_loop(0, deep // GROUP, step, 0)
        part = pl.ds(half * deep, deep)
        target = pl.ds(half * deep + (lats if first else 0), deep)
        stores += fetch([(spatial_ref.at[part], out_hbm.at[target])], out_sems.at[pl.ds(n, 1)])
    m = modes
    for part in range(2):
        at = 2 * part * m
        wide = wide_ref[at : at + m, :] + wide_ref[at + m : at + 2 * m, :]
        sums_ref[part * m : (part + 1) * m, :] = wide[:, :m] + wide[:, m:]
    for copy in stores:
        copy.wait()


def days_kernel(mine, core_ref, sums_ref, shelf_hbm, modes_hbm, ref, *refs):
    core = core_ref[0, 0]
    half = core if mine else 1 - core
    grid_ref, gram_ref, coded_ref, spatial_ref, sems = refs[-5:]
    lats, lons, modes = coded_ref.shape
    pairs = [(shelf_hbm.at[pl.ds(0, lats)], coded_ref), (modes_hbm.at[pl.ds((2 + half) * lats, lats)], spatial_ref)]
    loads = fetch(pairs, sems)
    spokes = ref.shape[0]
    many = PIECES * lats // spokes
    if mine:
        temporal = sums_ref[...]
    else:
        days = sums_ref.shape[0] - modes
        temporal = full(sums_ref[0:days, :], inverse_spd(add_ridge(sums_ref[days:, :])))
        refs[0][...] = temporal
    side = right_side(temporal)
    across = right_side(temporal.T)
    gram_ref[...] = full(temporal, temporal, (((0,), (0,)), ((), ())))

    for copy in loads:
        copy.wait()

    def step(g, _):
        at = g * many
        guess = times(split(jnp.concatenate([spatial_ref[at + p] for p in range(many)], axis=0)), across)
        coded = jnp.concatenate([coded_ref[g * many + p] for p in range(many)], axis=0)
        put_rows(ref, grid_ref, g, g * many, times(split(jnp.where(coded == GAP, guess, coded)), side))
        return _

    lax.fori_loop(0, spokes // PIECES, step, 0)
    put_block(half, grid_ref, gram_ref, ref)


def last_kernel(sums_ref, days_ref):
    days = days_ref.shape[0]
    days_ref[...] = full(sums_ref[0:days, :], inverse_spd(add_ridge(sums_ref[days:, :])))


SMEM = pl.BlockSpec(memory_space=pltpu.SMEM)
VMEM = pl.BlockSpec(memory_space=pltpu.VMEM)
HBM = pl.BlockSpec(memory_space=pltpu.HBM)


def call(kernel, outs, specs, scratch, name, flops, nbytes, room=60):
    return pl.pallas_call(
        kernel,
        out_shape=[jax.ShapeDtypeStruct(shape, f32) for shape, _ in outs],
        in_specs=specs,
        out_specs=[place for _, place in outs],
        scratch_shapes=[pltpu.VMEM(shape, f32) if isinstance(shape, tuple) else shape for shape in scratch],
        name=name,
        cost_estimate=pl.CostEstimate(flops=flops, bytes_accessed=nbytes, transcendentals=0),
        compiler_params=pltpu.CompilerParams(vmem_limit_bytes=room * 1024 * 1024),
    )


def copy_sems(count):
    return pltpu.SemaphoreType.DMA((count,))


def first_call(mine, core, anomaly, observed, mask, days, spokes):
    lats, lons, n = anomaly.shape
    block = (spokes, lats * lons // (2 * spokes) + 16, n)
    grid = (lats // 2, lons, n)
    scratch = [grid, (n, n), grid, pltpu.VMEM(grid, jnp.int32), pltpu.VMEM(mask.shape, jnp.int32), (n, n), grid, grid]
    scratch += [(lons, n), copy_sems(2 + 4 * (spokes // PIECES))]
    outs = [(block, VMEM), ((SHELF, lons, n), HBM)]
    specs = [SMEM] + [HBM] * 4
    return call(functools.partial(first_kernel, mine), outs, specs, scratch, "first_projection", 10**9, 10**7, FIRST_ROOM)(
        core, anomaly, observed, mask, days
    )


def modes_call(first, core, weight, here, there, days, shelves, lats):
    _, lons, n = shelves[0].shape
    half = (lats // 2, lons, n)
    grid = (lats, lons, n)
    outs = [((SHELF, lons, n) if first else grid, HBM), ((2 * n, n), VMEM)]
    scratch = [(lats + 2, lons, n), ((8 if first else 4) * lons, n), (4 * n, 2 * n), grid] + [half] * (6 if first else 4)
    scratch += [copy_sems(4), copy_sems(4)]
    specs = [SMEM, SMEM] + [VMEM] * 3 + [HBM] * len(shelves)
    return call(functools.partial(modes_kernel, first), outs, specs, scratch, "modes_sweep", 2 * 10**9, 10**7, ROOM)(
        core, weight, here, there, days, *shelves
    )


def days_call(mine, core, sums, shelf, modes, spokes, lats):
    _, lons, n = shelf.shape
    block = (spokes, lats * lons // (2 * spokes) + 16, n)
    outs = [(block, VMEM)] if mine else [(block, VMEM), ((sums.shape[0] - n, n), VMEM)]
    grid = (lats // 2, lons, n)
    scratch = [grid, (n, n), grid, grid, copy_sems(2)]
    return call(functools.partial(days_kernel, mine), outs, [SMEM, VMEM, HBM, HBM], scratch, "days_sweep", 2 * 10**9, 10**7, ROOM)(
        core, sums, shelf, modes
    )


def last_call(sums):
    n = sums.shape[1]
    return call(last_kernel, [((sums.shape[0] - n, n), VMEM)], [VMEM], [], "last_days", 10**7, 10**6, 16)(sums)[0]


def lat_weights(first_row, row_count, total_rows):
    index_rows = first_row + jnp.arange(row_count, dtype=jnp.float32)
    angle = (lat_south + lat_span * (index_rows + 0.5) / total_rows) * (math.pi / 180.0)
    cosine = jnp.cos(angle)
    return 1.0 / (cosine * cosine)


def swap_core(value):
    return lax.ppermute(value, "core", [(0, 1), (1, 0)])


def halo_pairs(lats, lons, spokes):
    pairs = []
    for la in range(lats):
        for lo in range(lons):
            for q in range(spokes):
                for core in range(2):
                    if q < spokes // 2:
                        to_la, to_lo = la + 2 * core - 1, lo
                    else:
                        to_la, to_lo = la, lo + (1 if q >= 3 * spokes // 4 else -1)
                    if 0 <= to_la < lats and 0 <= to_lo < lons:
                        here = ((la * lons + lo) * spokes + q) * 2 + core
                        there = ((to_la * lons + to_lo) * spokes + q) * 2 + core
                        pairs.append((here, there))
    return pairs


def gather_all(value, axes, size):
    spread = jnp.broadcast_to(value[None], (size,) + value.shape)
    return lax.all_to_all(spread, axes, 0, 0, tiled=True)


def sum_cells(value):
    size = lax.axis_size("lat") * lax.axis_size("lon")
    rows = value.shape[0]
    parts = lax.all_to_all(value.reshape(size, rows // size, -1), LL, 0, 0, tiled=True)
    mine = jnp.sum(parts, axis=0)
    return gather_all(mine, LL, size).reshape(rows, -1)


def edges_of(grid):
    middle = grid.shape[0] // 2
    up, down = grid[:middle], grid[middle:]
    return jnp.concatenate([up[0], up[:, 0], up[:, -1], down[-1], down[:, 0], down[:, -1]], axis=0)


def on_device(anomaly, observed, ocean_mask, start_days):
    rows_lat, cols_lon, _ = anomaly.shape
    rank_count = start_days.shape[1]
    lats, lons = lax.axis_size("lat"), lax.axis_size("lon")
    spokes = lax.axis_size("zlo") * lax.axis_size("y")
    core = lax.axis_index("core")
    spoke = lax.axis_index("zlo") * lax.axis_size("y") + lax.axis_index("y")
    pairs = halo_pairs(lats, lons, spokes)
    cells = rows_lat * cols_lon // (2 * spokes)
    core_word = core.reshape(1, 1).astype(jnp.int32)
    sea_grid = ocean_mask.astype(f32)
    first_lat = (lax.axis_index("lat") * rows_lat).astype(f32)
    weight = lat_weights(first_lat, rows_lat, float(rows_lat * lats)).reshape(1, rows_lat)
    edge_sea = lax.dynamic_slice_in_dim(edges_of(sea_grid), (core * spokes + spoke) * 8, 8)
    edge_sea = jnp.broadcast_to(edge_sea[:, None], (8, rank_count))
    temporal = start_days
    shelves = [None, None]
    other, shelves[1] = first_call(False, core_word, anomaly, observed, ocean_mask, start_days, spokes)
    mine, shelves[0] = first_call(True, core_word, anomaly, observed, ocean_mask, start_days, spokes)
    for sweep in range(ITERS):
        half = mine + swap_core(other)
        shard = jnp.sum(lax.all_to_all(half, YZ, 0, 0, tiled=True), axis=0)
        send = shard[cells : cells + 8]
        if sweep == 0:
            send = jnp.concatenate([send, edge_sea], axis=0)
        halo = lax.ppermute(send, ALL, pairs)
        shard = jnp.concatenate([shard[:cells], halo, shard[cells + 8 :]], axis=0)
        here = gather_all(shard, YZ, spokes)
        there = swap_core(here)
        spatial, sums = modes_call(sweep == 0, core_word, weight, here, there, temporal, shelves, rows_lat)
        sums = sum_cells(sums)
        if sweep == 0:
            shelves.append(spatial)
        if sweep < ITERS - 1:
            other, temporal = days_call(False, core_word, sums, shelves[1], spatial, spokes, rows_lat)
            (mine,) = days_call(True, core_word, temporal, shelves[0], spatial, spokes, rows_lat)
        else:
            temporal = last_call(sums)
    return (spatial, temporal)


def solution(mesh):
    lats, lons, days = mesh.devices.shape
    fine = Mesh(mesh.devices.reshape(lats, lons, 2, days // 4, 2), ALL)
    in_specs = (P("lat", "lon", DAY), P("lat", "lon", DAY), P("lat", "lon"), P(DAY, None))
    out_specs = (P("lat", "lon", None), P(DAY, None))
    return jax.shard_map(
        on_device, mesh=fine, in_specs=in_specs, out_specs=out_specs, check_vma=False
    )
```

```python
import functools
import math

import jax
import jax.numpy as jnp
from jax import lax
from jax.experimental import pallas as pl
from jax.experimental.pallas import tpu as pltpu
from jax.sharding import Mesh, PartitionSpec as P

ITERS = 2


ridge_term = 1.0
diffusion = 0.1
lat_south = 30.0
lat_span = 16.0

GAP = 1e30
PIECES = 8
GROUP = 16
FIRST_ROOM = 57
ROOM = 50
SHELF = 384
YZ = ("zlo", "y")
DAY = ("zlo", "y", "core")
ALL = ("lat", "lon", "zlo", "y", "core")
LL = ("lat", "lon")
f32, bf16 = jnp.float32, jnp.bfloat16


def inverse_spd(matrix):
    size = matrix.shape[0]
    blocks = [matrix[8 * r : 8 * r + 8] for r in range(size // 8)]
    lane = lax.broadcasted_iota(jnp.int32, (1, size), 1)
    row = lax.broadcasted_iota(jnp.int32, (8, size), 0)
    for k in range(0, size, 4):
        home, off = k // 8, k % 8
        rows = [blocks[home][off + i : off + i + 1] for i in range(4)]
        d = [[jnp.broadcast_to(rows[i][:, k + j : k + j + 1], (1, size)) for j in range(4)] for i in range(4)]
        in_panel = (lane >= k) & (lane < k + 4)
        a, b, c = d[0][0], d[0][1], d[1][1]
        r = 1.0 / (a * c - b * b)
        a00, a01, a11 = c * r, -b * r, a * r
        b02, b03, b12, b13 = d[0][2], d[0][3], d[1][2], d[1][3]
        g02, g03 = a00 * b02 + a01 * b12, a00 * b03 + a01 * b13
        g12, g13 = a01 * b02 + a11 * b12, a01 * b03 + a11 * b13
        s22 = d[2][2] - (b02 * g02 + b12 * g12)
        s23 = d[2][3] - (b02 * g03 + b12 * g13)
        s33 = d[3][3] - (b03 * g03 + b13 * g13)
        r = 1.0 / (s22 * s33 - s23 * s23)
        i22, i23, i33 = s33 * r, -s23 * r, s22 * r
        h02, h03 = g02 * i22 + g03 * i23, g02 * i23 + g03 * i33
        h12, h13 = g12 * i22 + g13 * i23, g12 * i23 + g13 * i33
        q00 = a00 + (h02 * g02 + h03 * g03)
        q01 = a01 + (h02 * g12 + h03 * g13)
        q11 = a11 + (h12 * g12 + h13 * g13)
        inv = [[q00, q01, -h02, -h03], [q01, q11, -h12, -h13], [-h02, -h12, i22, i23], [-h03, -h13, i23, i33]]
        unit = [jnp.where(lane == k + j, 1.0, jnp.where(in_panel, 0.0, rows[j])) for j in range(4)]
        new = [
            (inv[i][0] * unit[0] + inv[i][1] * unit[1]) + (inv[i][2] * unit[2] + inv[i][3] * unit[3])
            for i in range(4)
        ]
        out = []
        for r8, block in enumerate(blocks):
            cols = [block[:, k + j : k + j + 1] for j in range(4)]
            keep = jnp.where(in_panel, 0.0, block)
            keep = keep - ((cols[0] * new[0] + cols[1] * new[1]) + (cols[2] * new[2] + cols[3] * new[3]))
            if r8 == home:
                for j in range(4):
                    keep = jnp.where(row == off + j, new[j], keep)
            out.append(keep)
        blocks = out
    return jnp.concatenate(blocks, axis=0)


def add_ridge(gram):
    size = gram.shape[0]
    same = lax.broadcasted_iota(jnp.int32, (size, size), 0) == lax.broadcasted_iota(jnp.int32, (size, size), 1)
    return gram + jnp.where(same, ridge_term, 0.0)


def split(value):
    one = value.astype(bf16)
    return jnp.concatenate([one, (value - one.astype(f32)).astype(bf16)], axis=1)


def right_side(value):
    wide = split(value)
    return jnp.concatenate([wide, wide], axis=0)


def times(parts, side):
    wide = jnp.dot(parts, side, preferred_element_type=f32)
    n = wide.shape[1] // 2
    return wide[:, :n] + wide[:, n:]


def dot_tn(left, right):
    return lax.dot_general(left, right, (((0,), (0,)), ((), ())), preferred_element_type=f32)


def full(left, right, dims=(((1,), (0,)), ((), ()))):
    return lax.dot_general(left, right, dims, precision=lax.Precision.HIGHEST, preferred_element_type=f32)


def put_block(half, grid_ref, gram_ref, ref):
    lats, lons, modes = grid_ref.shape
    spokes = ref.shape[0]
    cells = lats * lons // spokes
    line = grid_ref[half * (lats - 1)]
    for q in range(spokes):
        if q < lons // 8:
            edge = line[8 * q : 8 * q + 8]
        else:
            side, at = divmod(8 * q - lons, lats)
            edge = grid_ref[at : at + 8, side * (lons - 1), :]
        ref[q, cells : cells + 8, :] = edge
        ref[q, cells + 8 : cells + 16, :] = gram_ref[8 * q : 8 * q + 8, :]


def put_rows(ref, grid_ref, g, base, out):
    lons = grid_ref.shape[1]
    cells = ref.shape[1] - 16
    for p in range(PIECES):
        ref[g * PIECES + p, 0:cells, :] = out[p * cells : (p + 1) * cells]
    for p in range(out.shape[0] // lons):
        grid_ref[base + p] = out[p * lons : (p + 1) * lons]


def fetch(pairs, sems):
    copies = [pltpu.make_async_copy(src, dst, sems.at[n]) for n, (src, dst) in enumerate(pairs)]
    for copy in copies:
        copy.start()
    return copies


def first_kernel(
    mine, core_ref, anomaly_hbm, observed_hbm, mask_hbm, days_hbm, ref, shelf_hbm,
    grid_ref, gram_ref, anomaly_ref, observed_ref, mask_ref, days_ref, coded_ref, sea_ref, seat_ref, sems,
):
    core = core_ref[0, 0]
    half = core if mine else 1 - core
    lats, lons, days = coded_ref.shape
    spokes = ref.shape[0]
    many = PIECES * lats // spokes
    groups = spokes // PIECES
    small = fetch([(days_hbm, days_ref), (mask_hbm, mask_ref)], sems)
    loads, stores = [], []
    for g in range(groups):
        away, near = pl.ds(half * lats + g * many, many), pl.ds(g * many, many)
        pairs = [(anomaly_hbm.at[away], anomaly_ref.at[near]), (observed_hbm.at[away], observed_ref.at[near])]
        loads.append(fetch(pairs, sems.at[pl.ds(2 + 2 * g, 2)]))
    small[0].wait()
    temporal = days_ref[...]
    side = right_side(temporal)
    gram_ref[...] = full(temporal, temporal, (((0,), (0,)), ((), ())))
    small[1].wait()
    mask = mask_ref[...].astype(f32)
    seat_ref[...] = jnp.concatenate([mask, jnp.zeros((days - mask.shape[0], lons), f32)], axis=0).T
    for g in range(groups):
        for copy in loads[g]:
            copy.wait()

        def step(_, carry, g=g):
            rows = []
            for p in range(many):
                here = g * many + p
                i = half * lats + here
                turned = pltpu.roll(seat_ref[...], lax.rem(days - i, days), 1)
                sea = jnp.broadcast_to(turned[:, :1], (lons, days))
                sea_ref[here] = sea
                seen = observed_ref[here] != 0
                known = jnp.where(seen, sea * anomaly_ref[here], 0.0)
                coded_ref[here] = jnp.where(seen | (sea == 0.0), known, GAP)
                rows.append(known)
            put_rows(ref, grid_ref, g, g * many, times(split(jnp.concatenate(rows, axis=0)), side))
            return carry

        step(0, 0)
        near = pl.ds(g * many, many)
        pairs = [(coded_ref.at[near], shelf_hbm.at[near]), (sea_ref.at[near], shelf_hbm.at[pl.ds(lats + g * many, many)])]
        stores += fetch(pairs, sems.at[pl.ds(2 + 2 * groups + 2 * g, 2)])
    put_block(half, grid_ref, gram_ref, ref)
    for copy in stores:
        copy.wait()


def modes_kernel(first, core_ref, weight_ref, here_ref, there_ref, here_late_ref, there_late_ref, inverse_ref, days_ref, *refs):
    shelves, refs = refs[0 : (2 if first else 3)], refs[(2 if first else 3) :]
    out_hbm, sums_ref, pad_ref, rim_ref, wide_ref, spatial_ref = refs[0:6]
    coded_refs, field_refs, refs = refs[6:8], refs[8:10], refs[10:]
    around_refs = refs[0:2] if first else field_refs
    in_sems, out_sems = refs[-2:]
    core = core_ref[0, 0]
    lats, lons, modes = spatial_ref.shape
    deep = lats // 2
    spokes = here_ref.shape[0]
    tiles = 2 if first else 1
    halves = (core, 1 - core)
    fields = [(shelves[n], deep) if first else (shelves[2], n * deep) for n in range(2)]
    pairs = [(shelf.at[pl.ds(at, deep)], field_refs[n]) for n, (shelf, at) in enumerate(fields)]
    pairs += [(shelves[n].at[pl.ds(0, deep)], coded_refs[n]) for n in range(2)]
    loads = fetch(pairs, in_sems)
    inverse_side = right_side(inverse_ref[...])
    days_side = right_side(days_ref[...].T)
    stores = []
    for half, early, late in ((core, here_ref, here_late_ref), (1 - core, there_ref, there_late_ref)):
        for q in range(spokes):
            at = half * deep + q * 2 + 1
            pad_ref[at] = early[q, 0:lons, :]
            pad_ref[at + 1] = late[q, 0:lons, :]
            if q < lons // 8:
                at = half * lons + 8 * q
            else:
                side, along = divmod(8 * q - lons, deep)
                at = 2 * lons + side * lats + half * deep + along
            for t in range(tiles):
                rim_ref[pl.ds(pl.multiple_of(t * 4 * lons + at, 8), 8), :] = late[q, lons + 8 * t : lons + 8 * t + 8, :]
    for copy in loads:
        copy.wait()
    pad_ref[0] = rim_ref[lons : 2 * lons, :]
    pad_ref[lats + 1] = rim_ref[0:lons, :]
    row = lax.broadcasted_iota(jnp.int32, (lons, modes), 0)

    def beside(value, i, kind):
        east = rim_ref[pl.ds(kind * 4 * lons + 2 * lons + i, 1), :]
        west = rim_ref[pl.ds(kind * 4 * lons + 2 * lons + lats + i, 1), :]
        ahead = jnp.where(row == lons - 1, east, pltpu.roll(value, lons - 1, 0))
        behind = jnp.where(row == 0, west, pltpu.roll(value, 1, 0))
        return ahead + behind

    if first:
        for n, half in enumerate(halves):
            field_ref, beyond_ref, around_ref = field_refs[n], field_refs[1 - n], around_refs[n]

            def masks(l, _, half=half, field_ref=field_ref, beyond_ref=beyond_ref, around_ref=around_ref):
                i = half * deep + l
                sea = field_ref[l]
                above = jnp.where(half == 0, rim_ref[5 * lons : 6 * lons, :], beyond_ref[deep - 1])
                below = jnp.where(half == 0, beyond_ref[0], rim_ref[4 * lons : 5 * lons, :])
                north = jnp.where(l == 0, above, field_ref[jnp.maximum(l - 1, 0)])
                south = jnp.where(l == deep - 1, below, field_ref[jnp.minimum(l + 1, deep - 1)])
                round_ = (north + south) + weight_ref[0, i] * beside(sea, i, 1)
                around_ref[l] = jnp.where(sea == 0.0, GAP, 1.0 - diffusion * round_)
                return _

            lax.fori_loop(0, deep, masks, 0, unroll=2)
            stores += fetch([(around_ref, out_hbm.at[pl.ds(n * deep, deep)])], out_sems.at[pl.ds(2 + n, 1)])

    wide_ref[...] = jnp.zeros_like(wide_ref)
    for n, half in enumerate(halves):

        def step(g, _, half=half, around_ref=around_refs[n], coded_ref=coded_refs[n]):
            smoothed = []
            for p in range(GROUP):
                l = g * GROUP + p
                i = half * deep + l
                around = around_ref[l]
                raw = pad_ref[i + 1]
                near = (pad_ref[i] + pad_ref[i + 2]) + weight_ref[0, i] * beside(raw, i, 0)
                smoothed.append(jnp.where(around == GAP, 0.0, around * raw + diffusion * near))
            spatial = times(split(jnp.concatenate(smoothed, axis=0)), inverse_side)
            parts = split(spatial)
            guess = times(parts, days_side)
            filled = []
            for p in range(GROUP):
                l = g * GROUP + p
                spatial_ref[half * deep + l] = spatial[p * lons : (p + 1) * lons]
                coded = coded_ref[l]
                filled.append(jnp.where(coded == GAP, guess[p * lons : (p + 1) * lons], coded))
            filled = split(jnp.concatenate(filled, axis=0))
            wide_ref[...] += dot_tn(jnp.concatenate([filled, parts], axis=1), parts)
            return _

        lax.fori_loop(0, deep // GROUP, step, 0)
        part = pl.ds(half * deep, deep)
        target = pl.ds(half * deep + (lats if first else 0), deep)
        stores += fetch([(spatial_ref.at[part], out_hbm.at[target])], out_sems.at[pl.ds(n, 1)])
    m = modes
    for part in range(2):
        at = 2 * part * m
        wide = wide_ref[at : at + m, :] + wide_ref[at + m : at + 2 * m, :]
        sums_ref[part * m : (part + 1) * m, :] = wide[:, :m] + wide[:, m:]
    for copy in stores:
        copy.wait()


def days_kernel(mine, core_ref, sums_ref, shelf_hbm, modes_hbm, ref, *refs):
    core = core_ref[0, 0]
    half = core if mine else 1 - core
    grid_ref, gram_ref, coded_ref, spatial_ref, sems = refs[-5:]
    lats, lons, modes = coded_ref.shape
    pairs = [(shelf_hbm.at[pl.ds(0, lats)], coded_ref), (modes_hbm.at[pl.ds((2 + half) * lats, lats)], spatial_ref)]
    loads = fetch(pairs, sems)
    spokes = ref.shape[0]
    many = PIECES * lats // spokes
    if mine:
        temporal = sums_ref[...]
    else:
        days = sums_ref.shape[0] - modes
        temporal = full(sums_ref[0:days, :], inverse_spd(add_ridge(sums_ref[days:, :])))
        refs[0][...] = temporal
    side = right_side(temporal)
    across = right_side(temporal.T)
    gram_ref[...] = full(temporal, temporal, (((0,), (0,)), ((), ())))

    for copy in loads:
        copy.wait()

    def step(g, _):
        at = g * many
        guess = times(split(jnp.concatenate([spatial_ref[at + p] for p in range(many)], axis=0)), across)
        coded = jnp.concatenate([coded_ref[g * many + p] for p in range(many)], axis=0)
        put_rows(ref, grid_ref, g, g * many, times(split(jnp.where(coded == GAP, guess, coded)), side))
        return _

    lax.fori_loop(0, spokes // PIECES, step, 0)
    put_block(half, grid_ref, gram_ref, ref)


def inverse_kernel(early_ref, inverse_ref):
    spokes, rows, _ = early_ref.shape
    gram = jnp.concatenate([early_ref[q, rows - 8 : rows, :] for q in range(spokes)], axis=0)
    inverse_ref[...] = inverse_spd(add_ridge(gram))


def last_kernel(sums_ref, days_ref):
    days = days_ref.shape[0]
    days_ref[...] = full(sums_ref[0:days, :], inverse_spd(add_ridge(sums_ref[days:, :])))


SMEM = pl.BlockSpec(memory_space=pltpu.SMEM)
VMEM = pl.BlockSpec(memory_space=pltpu.VMEM)
HBM = pl.BlockSpec(memory_space=pltpu.HBM)


def call(kernel, outs, specs, scratch, name, flops, nbytes, room=60):
    return pl.pallas_call(
        kernel,
        out_shape=[jax.ShapeDtypeStruct(shape, f32) for shape, _ in outs],
        in_specs=specs,
        out_specs=[place for _, place in outs],
        scratch_shapes=[pltpu.VMEM(shape, f32) if isinstance(shape, tuple) else shape for shape in scratch],
        name=name,
        cost_estimate=pl.CostEstimate(flops=flops, bytes_accessed=nbytes, transcendentals=0),
        compiler_params=pltpu.CompilerParams(vmem_limit_bytes=room * 1024 * 1024),
    )


def copy_sems(count):
    return pltpu.SemaphoreType.DMA((count,))


def first_call(mine, core, anomaly, observed, mask, days, spokes):
    lats, lons, n = anomaly.shape
    block = (spokes, lats * lons // (2 * spokes) + 16, n)
    grid = (lats // 2, lons, n)
    scratch = [grid, (n, n), grid, pltpu.VMEM(grid, jnp.int32), pltpu.VMEM(mask.shape, jnp.int32), (n, n), grid, grid]
    scratch += [(lons, n), copy_sems(2 + 4 * (spokes // PIECES))]
    outs = [(block, VMEM), ((SHELF, lons, n), HBM)]
    specs = [SMEM] + [HBM] * 4
    return call(functools.partial(first_kernel, mine), outs, specs, scratch, "first_projection", 10**9, 10**7, FIRST_ROOM)(
        core, anomaly, observed, mask, days
    )


def modes_call(first, core, weight, pieces, days, shelves, lats):
    _, lons, n = shelves[0].shape
    half = (lats // 2, lons, n)
    grid = (lats, lons, n)
    outs = [((SHELF, lons, n) if first else grid, HBM), ((2 * n, n), VMEM)]
    scratch = [(lats + 2, lons, n), ((8 if first else 4) * lons, n), (4 * n, 2 * n), grid] + [half] * (6 if first else 4)
    scratch += [copy_sems(4), copy_sems(4)]
    specs = [SMEM, SMEM] + [VMEM] * 6 + [HBM] * len(shelves)
    return call(functools.partial(modes_kernel, first), outs, specs, scratch, "modes_sweep", 2 * 10**9, 10**7, ROOM)(
        core, weight, *pieces, days, *shelves
    )


def days_call(mine, core, sums, shelf, modes, spokes, lats):
    _, lons, n = shelf.shape
    block = (spokes, lats * lons // (2 * spokes) + 16, n)
    outs = [(block, VMEM)] if mine else [(block, VMEM), ((sums.shape[0] - n, n), VMEM)]
    grid = (lats // 2, lons, n)
    scratch = [grid, (n, n), grid, grid, copy_sems(2)]
    return call(functools.partial(days_kernel, mine), outs, [SMEM, VMEM, HBM, HBM], scratch, "days_sweep", 2 * 10**9, 10**7, ROOM)(
        core, sums, shelf, modes
    )


def inverse_call(early):
    n = early.shape[2]
    return call(inverse_kernel, [((n, n), VMEM)], [VMEM], [], "days_inverse", 10**9, 2 * 10**7, 16)(early)[0]


def last_call(sums):
    n = sums.shape[1]
    return call(last_kernel, [((sums.shape[0] - n, n), VMEM)], [VMEM], [], "last_days", 10**7, 10**6, 16)(sums)[0]


def lat_weights(first_row, row_count, total_rows):
    index_rows = first_row + jnp.arange(row_count, dtype=jnp.float32)
    angle = (lat_south + lat_span * (index_rows + 0.5) / total_rows) * (math.pi / 180.0)
    cosine = jnp.cos(angle)
    return 1.0 / (cosine * cosine)


def swap_core(value):
    return lax.ppermute(value, "core", [(0, 1), (1, 0)])


def halo_pairs(lats, lons, spokes):
    pairs = []
    for la in range(lats):
        for lo in range(lons):
            for q in range(spokes):
                for core in range(2):
                    if q < spokes // 2:
                        to_la, to_lo = la + 2 * core - 1, lo
                    else:
                        to_la, to_lo = la, lo + (1 if q >= 3 * spokes // 4 else -1)
                    if 0 <= to_la < lats and 0 <= to_lo < lons:
                        here = ((la * lons + lo) * spokes + q) * 2 + core
                        there = ((to_la * lons + to_lo) * spokes + q) * 2 + core
                        pairs.append((here, there))
    return pairs


def gather_all(value, axes, size):
    spread = jnp.broadcast_to(value[None], (size,) + value.shape)
    return lax.all_to_all(spread, axes, 0, 0, tiled=True)


def sum_cells(value):
    size = lax.axis_size("lat") * lax.axis_size("lon")
    rows = value.shape[0]
    parts = lax.all_to_all(value.reshape(size, rows // size, -1), LL, 0, 0, tiled=True)
    mine = jnp.sum(parts, axis=0)
    return gather_all(mine, LL, size).reshape(rows, -1)


def edges_of(grid):
    middle = grid.shape[0] // 2
    up, down = grid[:middle], grid[middle:]
    return jnp.concatenate([up[0], up[:, 0], up[:, -1], down[-1], down[:, 0], down[:, -1]], axis=0)


def on_device(anomaly, observed, ocean_mask, start_days):
    rows_lat, cols_lon, _ = anomaly.shape
    rank_count = start_days.shape[1]
    lats, lons = lax.axis_size("lat"), lax.axis_size("lon")
    spokes = lax.axis_size("zlo") * lax.axis_size("y")
    core = lax.axis_index("core")
    spoke = lax.axis_index("zlo") * lax.axis_size("y") + lax.axis_index("y")
    pairs = halo_pairs(lats, lons, spokes)
    cells = rows_lat * cols_lon // (2 * spokes)
    core_word = core.reshape(1, 1).astype(jnp.int32)
    sea_grid = ocean_mask.astype(f32)
    first_lat = (lax.axis_index("lat") * rows_lat).astype(f32)
    weight = lat_weights(first_lat, rows_lat, float(rows_lat * lats)).reshape(1, rows_lat)
    edge_sea = lax.dynamic_slice_in_dim(edges_of(sea_grid), (core * spokes + spoke) * 8, 8)
    edge_sea = jnp.broadcast_to(edge_sea[:, None], (8, rank_count))
    temporal = start_days
    shelves = [None, None]
    other, shelves[1] = first_call(False, core_word, anomaly, observed, ocean_mask, start_days, spokes)
    mine, shelves[0] = first_call(True, core_word, anomaly, observed, ocean_mask, start_days, spokes)
    for sweep in range(ITERS):
        half = mine + swap_core(other)
        shard = jnp.sum(lax.all_to_all(half, YZ, 0, 0, tiled=True), axis=0)
        send = shard[cells : cells + 8]
        if sweep == 0:
            send = jnp.concatenate([send, edge_sea], axis=0)
        halo = lax.ppermute(send, ALL, pairs)
        early = gather_all(jnp.concatenate([shard[:cols_lon], shard[cells + 8 :]], axis=0), YZ, spokes)
        after = jnp.concatenate([shard[cols_lon:cells], halo], axis=0)
        early, after = lax.optimization_barrier((early, after))
        late = gather_all(after, YZ, spokes)
        there, inverse = swap_core(early), inverse_call(early)
        late, there, inverse = lax.optimization_barrier((late, there, inverse))
        pieces = (early, there, late, swap_core(late), inverse)
        spatial, sums = modes_call(sweep == 0, core_word, weight, pieces, temporal, shelves, rows_lat)
        sums = sum_cells(sums)
        if sweep == 0:
            shelves.append(spatial)
        if sweep < ITERS - 1:
            other, temporal = days_call(False, core_word, sums, shelves[1], spatial, spokes, rows_lat)
            (mine,) = days_call(True, core_word, temporal, shelves[0], spatial, spokes, rows_lat)
        else:
            temporal = last_call(sums)
    return (spatial, temporal)


def solution(mesh):
    lats, lons, days = mesh.devices.shape
    fine = Mesh(mesh.devices.reshape(lats, lons, 2, days // 4, 2), ALL)
    in_specs = (P("lat", "lon", DAY), P("lat", "lon", DAY), P("lat", "lon"), P(DAY, None))
    out_specs = (P("lat", "lon", None), P(DAY, None))
    return jax.shard_map(
        on_device, mesh=fine, in_specs=in_specs, out_specs=out_specs, check_vma=False
    )
```

```python
import functools
import math

import jax
import jax.numpy as jnp
from jax import lax
from jax.experimental import pallas as pl
from jax.experimental.pallas import tpu as pltpu
from jax.sharding import Mesh, PartitionSpec as P

ITERS = 2


ridge_term = 1.0
diffusion = 0.1
lat_south = 30.0
lat_span = 16.0

GAP = 1e30
PIECES = 8
DAYS_PIECES = 16
GROUP = 16
FIRST_ROOM = 57
ROOM = 50
SHELF = 384
YZ = ("zlo", "y")
DAY = ("zlo", "y", "core")
ALL = ("lat", "lon", "zlo", "y", "core")
LL = ("lat", "lon")
f32, bf16 = jnp.float32, jnp.bfloat16


def inverse_four(d):
    a, b, c = d[0][0], d[0][1], d[1][1]
    r = 1.0 / (a * c - b * b)
    a00, a01, a11 = c * r, -b * r, a * r
    b02, b03, b12, b13 = d[0][2], d[0][3], d[1][2], d[1][3]
    g02, g03 = a00 * b02 + a01 * b12, a00 * b03 + a01 * b13
    g12, g13 = a01 * b02 + a11 * b12, a01 * b03 + a11 * b13
    s22 = d[2][2] - (b02 * g02 + b12 * g12)
    s23 = d[2][3] - (b02 * g03 + b12 * g13)
    s33 = d[3][3] - (b03 * g03 + b13 * g13)
    r = 1.0 / (s22 * s33 - s23 * s23)
    i22, i23, i33 = s33 * r, -s23 * r, s22 * r
    h02, h03 = g02 * i22 + g03 * i23, g02 * i23 + g03 * i33
    h12, h13 = g12 * i22 + g13 * i23, g12 * i23 + g13 * i33
    q00 = a00 + (h02 * g02 + h03 * g03)
    q01 = a01 + (h02 * g12 + h03 * g13)
    q11 = a11 + (h12 * g12 + h13 * g13)
    return [[q00, q01, -h02, -h03], [q01, q11, -h12, -h13], [-h02, -h12, i22, i23], [-h03, -h13, i23, i33]]


def tree(terms):
    while len(terms) > 1:
        terms = [terms[i] + terms[i + 1] if i + 1 < len(terms) else terms[i] for i in range(0, len(terms), 2)]
    return terms[0]


def inverse_spd(matrix):
    size = matrix.shape[0]
    four = range(4)
    blocks = [matrix[8 * r : 8 * r + 8] for r in range(size // 8)]
    lane = lax.broadcasted_iota(jnp.int32, (8, size), 1)
    row = lax.broadcasted_iota(jnp.int32, (8, size), 0)
    for home in range(size // 8):
        k = 8 * home
        rows = [blocks[home][i : i + 1] for i in range(8)]
        d = [[jnp.broadcast_to(rows[min(i, j)][:, k + max(i, j) : k + max(i, j) + 1], (1, size)) for j in range(8)] for i in range(8)]
        top = inverse_four([[d[i][j] for j in four] for i in four])
        side = [[d[i][4 + j] for j in four] for i in four]
        g = [[tree([top[i][m] * side[m][j] for m in four]) for j in four] for i in four]
        s = [[None] * 4 for _ in four]
        for i in four:
            for j in range(i, 4):
                s[i][j] = s[j][i] = d[4 + i][4 + j] - tree([side[m][i] * g[m][j] for m in four])
        low = inverse_four(s)
        h = [[tree([g[i][m] * low[m][j] for m in four]) for j in four] for i in four]
        q = [[None] * 4 for _ in four]
        for i in four:
            for j in range(i, 4):
                q[i][j] = q[j][i] = top[i][j] + tree([h[i][m] * g[j][m] for m in four])
        inv = [q[i] + [-h[i][j] for j in four] for i in four] + [[-h[j][i] for j in four] + low[i] for i in four]
        in_panel = (lane >= k) & (lane < k + 8)
        unit = jnp.where(in_panel, jnp.where(lane == row + k, 1.0, 0.0), blocks[home])
        unit = [unit[i : i + 1] for i in range(8)]
        new = [tree([inv[i][j] * unit[j] for j in range(8)]) for i in range(8)]
        for r8, block in enumerate(blocks):
            if r8 != home:
                keep = jnp.where(in_panel, 0.0, block)
                blocks[r8] = keep - tree([block[:, k + j : k + j + 1] * new[j] for j in range(8)])
        blocks[home] = jnp.concatenate(new, axis=0)
    return jnp.concatenate(blocks, axis=0)


def add_ridge(gram):
    size = gram.shape[0]
    same = lax.broadcasted_iota(jnp.int32, (size, size), 0) == lax.broadcasted_iota(jnp.int32, (size, size), 1)
    return gram + jnp.where(same, ridge_term, 0.0)


def split(value):
    one = value.astype(bf16)
    return jnp.concatenate([one, (value - one.astype(f32)).astype(bf16)], axis=1)


def right_side(value):
    wide = split(value)
    return jnp.concatenate([wide, wide], axis=0)


def times(parts, side):
    wide = jnp.dot(parts, side, preferred_element_type=f32)
    n = wide.shape[1] // 2
    return wide[:, :n] + wide[:, n:]


def dot_tn(left, right):
    return lax.dot_general(left, right, (((0,), (0,)), ((), ())), preferred_element_type=f32)


def full(left, right, dims=(((1,), (0,)), ((), ()))):
    return lax.dot_general(left, right, dims, precision=lax.Precision.HIGHEST, preferred_element_type=f32)


def put_block(half, grid_ref, gram_ref, ref):
    lats, lons, modes = grid_ref.shape
    spokes = ref.shape[0]
    cells = lats * lons // spokes
    line = grid_ref[half * (lats - 1)]
    for q in range(spokes):
        if q < lons // 8:
            edge = line[8 * q : 8 * q + 8]
        else:
            side, at = divmod(8 * q - lons, lats)
            edge = grid_ref[at : at + 8, side * (lons - 1), :]
        ref[q, cells : cells + 8, :] = edge
        ref[q, cells + 8 : cells + 16, :] = gram_ref[8 * q : 8 * q + 8, :]


def put_rows(ref, grid_ref, g, base, out):
    lons = grid_ref.shape[1]
    cells = ref.shape[1] - 16
    pieces = out.shape[0] // cells
    for p in range(pieces):
        ref[g * pieces + p, 0:cells, :] = out[p * cells : (p + 1) * cells]
    for p in range(out.shape[0] // lons):
        grid_ref[base + p] = out[p * lons : (p + 1) * lons]


def fetch(pairs, sems):
    copies = [pltpu.make_async_copy(src, dst, sems.at[n]) for n, (src, dst) in enumerate(pairs)]
    for copy in copies:
        copy.start()
    return copies


def first_kernel(
    mine, core_ref, anomaly_hbm, observed_hbm, mask_hbm, days_hbm, ref, shelf_hbm,
    grid_ref, gram_ref, anomaly_ref, observed_ref, mask_ref, days_ref, coded_ref, sea_ref, seat_ref, sems,
):
    core = core_ref[0, 0]
    half = core if mine else 1 - core
    lats, lons, days = coded_ref.shape
    spokes = ref.shape[0]
    many = PIECES * lats // spokes
    groups = spokes // PIECES
    small = fetch([(days_hbm, days_ref), (mask_hbm, mask_ref)], sems)
    loads, stores = [], []
    for g in range(groups):
        away, near = pl.ds(half * lats + g * many, many), pl.ds(g * many, many)
        pairs = [(anomaly_hbm.at[away], anomaly_ref.at[near]), (observed_hbm.at[away], observed_ref.at[near])]
        loads.append(fetch(pairs, sems.at[pl.ds(2 + 2 * g, 2)]))
    small[0].wait()
    temporal = days_ref[...]
    side = right_side(temporal)
    gram_ref[...] = full(temporal, temporal, (((0,), (0,)), ((), ())))
    small[1].wait()
    mask = mask_ref[...].astype(f32)
    seat_ref[...] = jnp.concatenate([mask, jnp.zeros((days - mask.shape[0], lons), f32)], axis=0).T
    for g in range(groups):
        for copy in loads[g]:
            copy.wait()

        def step(_, carry, g=g):
            rows = []
            for p in range(many):
                here = g * many + p
                i = half * lats + here
                turned = pltpu.roll(seat_ref[...], lax.rem(days - i, days), 1)
                sea = jnp.broadcast_to(turned[:, :1], (lons, days))
                sea_ref[here] = sea
                seen = observed_ref[here] != 0
                known = jnp.where(seen, sea * anomaly_ref[here], 0.0)
                coded_ref[here] = jnp.where(seen | (sea == 0.0), known, GAP)
                rows.append(known)
            put_rows(ref, grid_ref, g, g * many, times(split(jnp.concatenate(rows, axis=0)), side))
            return carry

        step(0, 0)
        near = pl.ds(g * many, many)
        pairs = [(coded_ref.at[near], shelf_hbm.at[near]), (sea_ref.at[near], shelf_hbm.at[pl.ds(lats + g * many, many)])]
        stores += fetch(pairs, sems.at[pl.ds(2 + 2 * groups + 2 * g, 2)])
    put_block(half, grid_ref, gram_ref, ref)
    for copy in stores:
        copy.wait()


def modes_kernel(first, core_ref, weight_ref, here_ref, there_ref, days_ref, *refs):
    shelves, refs = refs[0 : (2 if first else 3)], refs[(2 if first else 3) :]
    out_hbm, sums_ref, pad_ref, rim_ref, wide_ref, spatial_ref = refs[0:6]
    coded_refs, field_refs, refs = refs[6:8], refs[8:10], refs[10:]
    around_refs = refs[0:2] if first else field_refs
    in_sems, out_sems = refs[-2:]
    core = core_ref[0, 0]
    lats, lons, modes = spatial_ref.shape
    deep = lats // 2
    spokes = here_ref.shape[0]
    per = deep // spokes
    cells = per * lons
    tiles = 2 if first else 1
    gram_at = cells + 8 * tiles
    halves = (core, 1 - core)
    fields = [(shelves[n], deep) if first else (shelves[2], n * deep) for n in range(2)]
    pairs = [(shelf.at[pl.ds(at, deep)], field_refs[n]) for n, (shelf, at) in enumerate(fields)]
    pairs += [(shelves[n].at[pl.ds(0, deep)], coded_refs[n]) for n in range(2)]
    loads = fetch(pairs, in_sems)
    gram = jnp.concatenate([here_ref[q, gram_at : gram_at + 8, :] for q in range(spokes)], axis=0)
    inverse_side = right_side(inverse_spd(add_ridge(gram)))
    days_side = right_side(days_ref[...].T)
    for copy in loads:
        copy.wait()
    stores = []

    for half, ref in zip(halves, (here_ref, there_ref)):
        for q in range(spokes):
            for p in range(per):
                pad_ref[half * deep + q * per + p + 1] = ref[q, p * lons : (p + 1) * lons, :]
            if q < lons // 8:
                at = half * lons + 8 * q
            else:
                side, along = divmod(8 * q - lons, deep)
                at = 2 * lons + side * lats + half * deep + along
            for t in range(tiles):
                rim_ref[pl.ds(pl.multiple_of(t * 4 * lons + at, 8), 8), :] = ref[q, cells + 8 * t : cells + 8 * t + 8, :]
    pad_ref[0] = rim_ref[lons : 2 * lons, :]
    pad_ref[lats + 1] = rim_ref[0:lons, :]
    row = lax.broadcasted_iota(jnp.int32, (lons, modes), 0)

    def beside(value, i, kind):
        east = rim_ref[pl.ds(kind * 4 * lons + 2 * lons + i, 1), :]
        west = rim_ref[pl.ds(kind * 4 * lons + 2 * lons + lats + i, 1), :]
        ahead = jnp.where(row == lons - 1, east, pltpu.roll(value, lons - 1, 0))
        behind = jnp.where(row == 0, west, pltpu.roll(value, 1, 0))
        return ahead + behind

    if first:
        for n, half in enumerate(halves):
            field_ref, beyond_ref, around_ref = field_refs[n], field_refs[1 - n], around_refs[n]

            def masks(l, _, half=half, field_ref=field_ref, beyond_ref=beyond_ref, around_ref=around_ref):
                i = half * deep + l
                sea = field_ref[l]
                above = jnp.where(half == 0, rim_ref[5 * lons : 6 * lons, :], beyond_ref[deep - 1])
                below = jnp.where(half == 0, beyond_ref[0], rim_ref[4 * lons : 5 * lons, :])
                north = jnp.where(l == 0, above, field_ref[jnp.maximum(l - 1, 0)])
                south = jnp.where(l == deep - 1, below, field_ref[jnp.minimum(l + 1, deep - 1)])
                round_ = (north + south) + weight_ref[0, i] * beside(sea, i, 1)
                around_ref[l] = jnp.where(sea == 0.0, GAP, 1.0 - diffusion * round_)
                return _

            lax.fori_loop(0, deep, masks, 0, unroll=2)
            stores += fetch([(around_ref, out_hbm.at[pl.ds(n * deep, deep)])], out_sems.at[pl.ds(2 + n, 1)])

    wide_ref[...] = jnp.zeros_like(wide_ref)
    for n, half in enumerate(halves):

        def step(g, _, half=half, around_ref=around_refs[n], coded_ref=coded_refs[n]):
            smoothed = []
            for p in range(GROUP):
                l = g * GROUP + p
                i = half * deep + l
                around = around_ref[l]
                raw = pad_ref[i + 1]
                near = (pad_ref[i] + pad_ref[i + 2]) + weight_ref[0, i] * beside(raw, i, 0)
                smoothed.append(jnp.where(around == GAP, 0.0, around * raw + diffusion * near))
            spatial = times(split(jnp.concatenate(smoothed, axis=0)), inverse_side)
            parts = split(spatial)
            guess = times(parts, days_side)
            filled = []
            for p in range(GROUP):
                l = g * GROUP + p
                spatial_ref[half * deep + l] = spatial[p * lons : (p + 1) * lons]
                coded = coded_ref[l]
                filled.append(jnp.where(coded == GAP, guess[p * lons : (p + 1) * lons], coded))
            filled = split(jnp.concatenate(filled, axis=0))
            wide_ref[...] += dot_tn(jnp.concatenate([filled, parts], axis=1), parts)
            return _

        lax.fori_loop(0, deep // GROUP, step, 0)
        part = pl.ds(half * deep, deep)
        target = pl.ds(half * deep + (lats if first else 0), deep)
        stores += fetch([(spatial_ref.at[part], out_hbm.at[target])], out_sems.at[pl.ds(n, 1)])
    m = modes
    for part in range(2):
        at = 2 * part * m
        wide = wide_ref[at : at + m, :] + wide_ref[at + m : at + 2 * m, :]
        sums_ref[part * m : (part + 1) * m, :] = wide[:, :m] + wide[:, m:]
    for copy in stores:
        copy.wait()


def days_kernel(mine, core_ref, sums_ref, shelf_hbm, modes_hbm, ref, *refs):
    core = core_ref[0, 0]
    half = core if mine else 1 - core
    grid_ref, gram_ref, coded_ref, spatial_ref, sems = refs[-5:]
    lats, lons, modes = coded_ref.shape
    pairs = [(shelf_hbm.at[pl.ds(0, lats)], coded_ref), (modes_hbm.at[pl.ds((2 + half) * lats, lats)], spatial_ref)]
    loads = fetch(pairs, sems)
    spokes = ref.shape[0]
    many = DAYS_PIECES * lats // spokes
    if mine:
        temporal = sums_ref[...]
    else:
        days = sums_ref.shape[0] - modes
        temporal = full(sums_ref[0:days, :], inverse_spd(add_ridge(sums_ref[days:, :])))
        refs[0][...] = temporal
    side = right_side(temporal)
    across = right_side(temporal.T)
    gram_ref[...] = full(temporal, temporal, (((0,), (0,)), ((), ())))

    for copy in loads:
        copy.wait()

    def step(g, _):
        at = g * many
        guess = times(split(jnp.concatenate([spatial_ref[at + p] for p in range(many)], axis=0)), across)
        coded = jnp.concatenate([coded_ref[g * many + p] for p in range(many)], axis=0)
        put_rows(ref, grid_ref, g, g * many, times(split(jnp.where(coded == GAP, guess, coded)), side))
        return _

    lax.fori_loop(0, spokes // DAYS_PIECES, step, 0)
    put_block(half, grid_ref, gram_ref, ref)


def last_kernel(sums_ref, days_ref):
    days = days_ref.shape[0]
    days_ref[...] = full(sums_ref[0:days, :], inverse_spd(add_ridge(sums_ref[days:, :])))


SMEM = pl.BlockSpec(memory_space=pltpu.SMEM)
VMEM = pl.BlockSpec(memory_space=pltpu.VMEM)
HBM = pl.BlockSpec(memory_space=pltpu.HBM)


def call(kernel, outs, specs, scratch, name, flops, nbytes, room=60):
    return pl.pallas_call(
        kernel,
        out_shape=[jax.ShapeDtypeStruct(shape, f32) for shape, _ in outs],
        in_specs=specs,
        out_specs=[place for _, place in outs],
        scratch_shapes=[pltpu.VMEM(shape, f32) if isinstance(shape, tuple) else shape for shape in scratch],
        name=name,
        cost_estimate=pl.CostEstimate(flops=flops, bytes_accessed=nbytes, transcendentals=0),
        compiler_params=pltpu.CompilerParams(vmem_limit_bytes=room * 1024 * 1024),
    )


def copy_sems(count):
    return pltpu.SemaphoreType.DMA((count,))


def first_call(mine, core, anomaly, observed, mask, days, spokes):
    lats, lons, n = anomaly.shape
    block = (spokes, lats * lons // (2 * spokes) + 16, n)
    grid = (lats // 2, lons, n)
    scratch = [grid, (n, n), grid, pltpu.VMEM(grid, jnp.int32), pltpu.VMEM(mask.shape, jnp.int32), (n, n), grid, grid]
    scratch += [(lons, n), copy_sems(2 + 4 * (spokes // PIECES))]
    outs = [(block, VMEM), ((SHELF, lons, n), HBM)]
    specs = [SMEM] + [HBM] * 4
    return call(functools.partial(first_kernel, mine), outs, specs, scratch, "first_projection", 10**9, 10**7, FIRST_ROOM)(
        core, anomaly, observed, mask, days
    )


def modes_call(first, core, weight, here, there, days, shelves, lats):
    _, lons, n = shelves[0].shape
    half = (lats // 2, lons, n)
    grid = (lats, lons, n)
    outs = [((SHELF, lons, n) if first else grid, HBM), ((2 * n, n), VMEM)]
    scratch = [(lats + 2, lons, n), ((8 if first else 4) * lons, n), (4 * n, 2 * n), grid] + [half] * (6 if first else 4)
    scratch += [copy_sems(4), copy_sems(4)]
    specs = [SMEM, SMEM] + [VMEM] * 3 + [HBM] * len(shelves)
    return call(functools.partial(modes_kernel, first), outs, specs, scratch, "modes_sweep", 2 * 10**9, 10**7, ROOM)(
        core, weight, here, there, days, *shelves
    )


def days_call(mine, core, sums, shelf, modes, spokes, lats):
    _, lons, n = shelf.shape
    block = (spokes, lats * lons // (2 * spokes) + 16, n)
    outs = [(block, VMEM)] if mine else [(block, VMEM), ((sums.shape[0] - n, n), VMEM)]
    grid = (lats // 2, lons, n)
    scratch = [grid, (n, n), grid, grid, copy_sems(2)]
    return call(functools.partial(days_kernel, mine), outs, [SMEM, VMEM, HBM, HBM], scratch, "days_sweep", 2 * 10**9, 10**7, ROOM)(
        core, sums, shelf, modes
    )


def last_call(sums):
    n = sums.shape[1]
    return call(last_kernel, [((sums.shape[0] - n, n), VMEM)], [VMEM], [], "last_days", 10**7, 10**6, 16)(sums)[0]


def lat_weights(first_row, row_count, total_rows):
    index_rows = first_row + jnp.arange(row_count, dtype=jnp.float32)
    angle = (lat_south + lat_span * (index_rows + 0.5) / total_rows) * (math.pi / 180.0)
    cosine = jnp.cos(angle)
    return 1.0 / (cosine * cosine)


def swap_core(value):
    return lax.ppermute(value, "core", [(0, 1), (1, 0)])


def halo_pairs(lats, lons, spokes):
    pairs = []
    for la in range(lats):
        for lo in range(lons):
            for q in range(spokes):
                for core in range(2):
                    if q < spokes // 2:
                        to_la, to_lo = la + 2 * core - 1, lo
                    else:
                        to_la, to_lo = la, lo + (1 if q >= 3 * spokes // 4 else -1)
                    if 0 <= to_la < lats and 0 <= to_lo < lons:
                        here = ((la * lons + lo) * spokes + q) * 2 + core
                        there = ((to_la * lons + to_lo) * spokes + q) * 2 + core
                        pairs.append((here, there))
    return pairs


def gather_all(value, axes, size):
    spread = jnp.broadcast_to(value[None], (size,) + value.shape)
    return lax.all_to_all(spread, axes, 0, 0, tiled=True)


def sum_cells(value):
    size = lax.axis_size("lat") * lax.axis_size("lon")
    rows = value.shape[0]
    parts = lax.all_to_all(value.reshape(size, rows // size, -1), LL, 0, 0, tiled=True)
    mine = jnp.sum(parts, axis=0)
    return gather_all(mine, LL, size).reshape(rows, -1)


def edges_of(grid):
    middle = grid.shape[0] // 2
    up, down = grid[:middle], grid[middle:]
    return jnp.concatenate([up[0], up[:, 0], up[:, -1], down[-1], down[:, 0], down[:, -1]], axis=0)


def on_device(anomaly, observed, ocean_mask, start_days):
    rows_lat, cols_lon, _ = anomaly.shape
    rank_count = start_days.shape[1]
    lats, lons = lax.axis_size("lat"), lax.axis_size("lon")
    spokes = lax.axis_size("zlo") * lax.axis_size("y")
    core = lax.axis_index("core")
    spoke = lax.axis_index("zlo") * lax.axis_size("y") + lax.axis_index("y")
    pairs = halo_pairs(lats, lons, spokes)
    cells = rows_lat * cols_lon // (2 * spokes)
    core_word = core.reshape(1, 1).astype(jnp.int32)
    sea_grid = ocean_mask.astype(f32)
    first_lat = (lax.axis_index("lat") * rows_lat).astype(f32)
    weight = lat_weights(first_lat, rows_lat, float(rows_lat * lats)).reshape(1, rows_lat)
    edge_sea = lax.dynamic_slice_in_dim(edges_of(sea_grid), (core * spokes + spoke) * 8, 8)
    edge_sea = jnp.broadcast_to(edge_sea[:, None], (8, rank_count))
    temporal = start_days
    shelves = [None, None]
    other, shelves[1] = first_call(False, core_word, anomaly, observed, ocean_mask, start_days, spokes)
    mine, shelves[0] = first_call(True, core_word, anomaly, observed, ocean_mask, start_days, spokes)
    for sweep in range(ITERS):
        half = mine + swap_core(other)
        shard = jnp.sum(lax.all_to_all(half, YZ, 0, 0, tiled=True), axis=0)
        send = shard[cells : cells + 8]
        if sweep == 0:
            send = jnp.concatenate([send, edge_sea], axis=0)
        halo = lax.ppermute(send, ALL, pairs)
        shard = jnp.concatenate([shard[:cells], halo, shard[cells + 8 :]], axis=0)
        here = gather_all(shard, YZ, spokes)
        there = swap_core(here)
        spatial, sums = modes_call(sweep == 0, core_word, weight, here, there, temporal, shelves, rows_lat)
        sums = sum_cells(sums)
        if sweep == 0:
            shelves.append(spatial)
        if sweep < ITERS - 1:
            other, temporal = days_call(False, core_word, sums, shelves[1], spatial, spokes, rows_lat)
            (mine,) = days_call(True, core_word, temporal, shelves[0], spatial, spokes, rows_lat)
        else:
            temporal = last_call(sums)
    return (spatial, temporal)


def solution(mesh):
    lats, lons, days = mesh.devices.shape
    fine = Mesh(mesh.devices.reshape(lats, lons, 2, days // 4, 2), ALL)
    in_specs = (P("lat", "lon", DAY), P("lat", "lon", DAY), P("lat", "lon"), P(DAY, None))
    out_specs = (P("lat", "lon", None), P(DAY, None))
    return jax.shard_map(
        on_device, mesh=fine, in_specs=in_specs, out_specs=out_specs, check_vma=False
    )
```

```python
import functools
import math

import jax
import jax.numpy as jnp
from jax import lax
from jax.experimental import pallas as pl
from jax.experimental.pallas import tpu as pltpu
from jax.sharding import Mesh, PartitionSpec as P

ITERS = 2


ridge_term = 1.0
diffusion = 0.1
lat_south = 30.0
lat_span = 16.0

GAP = 1e30
PIECES = 8
DAYS_PIECES = 16
GROUP = 32
FIRST_ROOM = 57
ROOM = 50
SHELF = 384
YZ = ("zlo", "y")
DAY = ("zlo", "y", "core")
ALL = ("lat", "lon", "zlo", "y", "core")
LL = ("lat", "lon")
f32, bf16 = jnp.float32, jnp.bfloat16


def inverse_four(d):
    a, b, c = d[0][0], d[0][1], d[1][1]
    r = 1.0 / (a * c - b * b)
    a00, a01, a11 = c * r, -b * r, a * r
    b02, b03, b12, b13 = d[0][2], d[0][3], d[1][2], d[1][3]
    g02, g03 = a00 * b02 + a01 * b12, a00 * b03 + a01 * b13
    g12, g13 = a01 * b02 + a11 * b12, a01 * b03 + a11 * b13
    s22 = d[2][2] - (b02 * g02 + b12 * g12)
    s23 = d[2][3] - (b02 * g03 + b12 * g13)
    s33 = d[3][3] - (b03 * g03 + b13 * g13)
    r = 1.0 / (s22 * s33 - s23 * s23)
    i22, i23, i33 = s33 * r, -s23 * r, s22 * r
    h02, h03 = g02 * i22 + g03 * i23, g02 * i23 + g03 * i33
    h12, h13 = g12 * i22 + g13 * i23, g12 * i23 + g13 * i33
    q00 = a00 + (h02 * g02 + h03 * g03)
    q01 = a01 + (h02 * g12 + h03 * g13)
    q11 = a11 + (h12 * g12 + h13 * g13)
    return [[q00, q01, -h02, -h03], [q01, q11, -h12, -h13], [-h02, -h12, i22, i23], [-h03, -h13, i23, i33]]


def tree(terms):
    while len(terms) > 1:
        terms = [terms[i] + terms[i + 1] if i + 1 < len(terms) else terms[i] for i in range(0, len(terms), 2)]
    return terms[0]


def inverse_spd(matrix):
    size = matrix.shape[0]
    four = range(4)
    blocks = [matrix[8 * r : 8 * r + 8] for r in range(size // 8)]
    lane = lax.broadcasted_iota(jnp.int32, (8, size), 1)
    row = lax.broadcasted_iota(jnp.int32, (8, size), 0)
    for home in range(size // 8):
        k = 8 * home
        rows = [blocks[home][i : i + 1] for i in range(8)]
        d = [[jnp.broadcast_to(rows[min(i, j)][:, k + max(i, j) : k + max(i, j) + 1], (1, size)) for j in range(8)] for i in range(8)]
        top = inverse_four([[d[i][j] for j in four] for i in four])
        side = [[d[i][4 + j] for j in four] for i in four]
        g = [[tree([top[i][m] * side[m][j] for m in four]) for j in four] for i in four]
        s = [[None] * 4 for _ in four]
        for i in four:
            for j in range(i, 4):
                s[i][j] = s[j][i] = d[4 + i][4 + j] - tree([side[m][i] * g[m][j] for m in four])
        low = inverse_four(s)
        h = [[tree([g[i][m] * low[m][j] for m in four]) for j in four] for i in four]
        q = [[None] * 4 for _ in four]
        for i in four:
            for j in range(i, 4):
                q[i][j] = q[j][i] = top[i][j] + tree([h[i][m] * g[j][m] for m in four])
        inv = [q[i] + [-h[i][j] for j in four] for i in four] + [[-h[j][i] for j in four] + low[i] for i in four]
        in_panel = (lane >= k) & (lane < k + 8)
        unit = jnp.where(in_panel, jnp.where(lane == row + k, 1.0, 0.0), blocks[home])
        unit = [unit[i : i + 1] for i in range(8)]
        new = [tree([inv[i][j] * unit[j] for j in range(8)]) for i in range(8)]
        for r8, block in enumerate(blocks):
            if r8 != home:
                keep = jnp.where(in_panel, 0.0, block)
                blocks[r8] = keep - tree([block[:, k + j : k + j + 1] * new[j] for j in range(8)])
        blocks[home] = jnp.concatenate(new, axis=0)
    return jnp.concatenate(blocks, axis=0)


def add_ridge(gram):
    size = gram.shape[0]
    same = lax.broadcasted_iota(jnp.int32, (size, size), 0) == lax.broadcasted_iota(jnp.int32, (size, size), 1)
    return gram + jnp.where(same, ridge_term, 0.0)


def split(value):
    one = value.astype(bf16)
    return jnp.concatenate([one, (value - one.astype(f32)).astype(bf16)], axis=1)


def right_side(value):
    wide = split(value)
    return jnp.concatenate([wide, wide], axis=0)


def times(parts, side):
    wide = jnp.dot(parts, side, preferred_element_type=f32)
    n = wide.shape[1] // 2
    return wide[:, :n] + wide[:, n:]


def dot_tn(left, right):
    return lax.dot_general(left, right, (((0,), (0,)), ((), ())), preferred_element_type=f32)


def full(left, right, dims=(((1,), (0,)), ((), ()))):
    return lax.dot_general(left, right, dims, precision=lax.Precision.HIGHEST, preferred_element_type=f32)


def put_block(half, grid_ref, gram_ref, ref):
    lats, lons, modes = grid_ref.shape
    spokes = ref.shape[0]
    cells = lats * lons // spokes
    line = grid_ref[half * (lats - 1)]
    for q in range(spokes):
        if q < lons // 8:
            edge = line[8 * q : 8 * q + 8]
        else:
            side, at = divmod(8 * q - lons, lats)
            edge = grid_ref[at : at + 8, side * (lons - 1), :]
        ref[q, cells : cells + 8, :] = edge
        ref[q, cells + 8 : cells + 16, :] = gram_ref[8 * q : 8 * q + 8, :]


def put_rows(ref, grid_ref, g, base, out):
    lons = grid_ref.shape[1]
    cells = ref.shape[1] - 16
    pieces = out.shape[0] // cells
    for p in range(pieces):
        ref[g * pieces + p, 0:cells, :] = out[p * cells : (p + 1) * cells]
    for p in range(out.shape[0] // lons):
        grid_ref[base + p] = out[p * lons : (p + 1) * lons]


def fetch(pairs, sems):
    copies = [pltpu.make_async_copy(src, dst, sems.at[n]) for n, (src, dst) in enumerate(pairs)]
    for copy in copies:
        copy.start()
    return copies


def first_kernel(
    mine, core_ref, anomaly_hbm, observed_hbm, mask_hbm, days_hbm, ref, shelf_hbm,
    grid_ref, gram_ref, anomaly_ref, observed_ref, mask_ref, days_ref, coded_ref, sea_ref, seat_ref, sems,
):
    core = core_ref[0, 0]
    half = core if mine else 1 - core
    lats, lons, days = coded_ref.shape
    spokes = ref.shape[0]
    many = PIECES * lats // spokes
    groups = spokes // PIECES
    small = fetch([(days_hbm, days_ref), (mask_hbm, mask_ref)], sems)
    loads, stores = [], []
    for g in range(groups):
        away, near = pl.ds(half * lats + g * many, many), pl.ds(g * many, many)
        pairs = [(anomaly_hbm.at[away], anomaly_ref.at[near]), (observed_hbm.at[away], observed_ref.at[near])]
        loads.append(fetch(pairs, sems.at[pl.ds(2 + 2 * g, 2)]))
    small[0].wait()
    temporal = days_ref[...]
    side = right_side(temporal)
    gram_ref[...] = full(temporal, temporal, (((0,), (0,)), ((), ())))
    small[1].wait()
    mask = mask_ref[...].astype(f32)
    seat_ref[...] = jnp.concatenate([mask, jnp.zeros((days - mask.shape[0], lons), f32)], axis=0).T
    for g in range(groups):
        for copy in loads[g]:
            copy.wait()

        def step(_, carry, g=g):
            rows = []
            for p in range(many):
                here = g * many + p
                i = half * lats + here
                turned = pltpu.roll(seat_ref[...], lax.rem(days - i, days), 1)
                sea = jnp.broadcast_to(turned[:, :1], (lons, days))
                sea_ref[here] = sea
                seen = observed_ref[here] != 0
                known = jnp.where(seen, sea * anomaly_ref[here], 0.0)
                coded_ref[here] = jnp.where(seen | (sea == 0.0), known, GAP)
                rows.append(known)
            put_rows(ref, grid_ref, g, g * many, times(split(jnp.concatenate(rows, axis=0)), side))
            return carry

        step(0, 0)
        near = pl.ds(g * many, many)
        pairs = [(coded_ref.at[near], shelf_hbm.at[near]), (sea_ref.at[near], shelf_hbm.at[pl.ds(lats + g * many, many)])]
        stores += fetch(pairs, sems.at[pl.ds(2 + 2 * groups + 2 * g, 2)])
    put_block(half, grid_ref, gram_ref, ref)
    for copy in stores:
        copy.wait()


def modes_kernel(first, core_ref, weight_ref, here_ref, there_ref, days_ref, *refs):
    shelves, refs = refs[0 : (2 if first else 3)], refs[(2 if first else 3) :]
    out_hbm, sums_ref, pad_ref, rim_ref, wide_ref, spatial_ref = refs[0:6]
    coded_refs, field_refs, refs = refs[6:8], refs[8:10], refs[10:]
    around_refs = refs[0:2] if first else field_refs
    in_sems, out_sems = refs[-2:]
    core = core_ref[0, 0]
    lats, lons, modes = spatial_ref.shape
    deep = lats // 2
    spokes = here_ref.shape[0]
    per = deep // spokes
    cells = per * lons
    tiles = 2 if first else 1
    gram_at = cells + 8 * tiles
    halves = (core, 1 - core)
    fields = [(shelves[n], deep) if first else (shelves[2], n * deep) for n in range(2)]
    pairs = [(shelf.at[pl.ds(at, deep)], field_refs[n]) for n, (shelf, at) in enumerate(fields)]
    pairs += [(shelves[n].at[pl.ds(0, deep)], coded_refs[n]) for n in range(2)]
    loads = fetch(pairs, in_sems)
    gram = jnp.concatenate([here_ref[q, gram_at : gram_at + 8, :] for q in range(spokes)], axis=0)
    inverse_side = right_side(inverse_spd(add_ridge(gram)))
    days_side = right_side(days_ref[...].T)
    for copy in loads:
        copy.wait()
    stores = []

    for half, ref in zip(halves, (here_ref, there_ref)):
        for q in range(spokes):
            for p in range(per):
                pad_ref[half * deep + q * per + p + 1] = ref[q, p * lons : (p + 1) * lons, :]
            if q < lons // 8:
                at = half * lons + 8 * q
            else:
                side, along = divmod(8 * q - lons, deep)
                at = 2 * lons + side * lats + half * deep + along
            for t in range(tiles):
                rim_ref[pl.ds(pl.multiple_of(t * 4 * lons + at, 8), 8), :] = ref[q, cells + 8 * t : cells + 8 * t + 8, :]
    pad_ref[0] = rim_ref[lons : 2 * lons, :]
    pad_ref[lats + 1] = rim_ref[0:lons, :]
    row = lax.broadcasted_iota(jnp.int32, (lons, modes), 0)

    def beside(value, i, kind):
        east = rim_ref[pl.ds(kind * 4 * lons + 2 * lons + i, 1), :]
        west = rim_ref[pl.ds(kind * 4 * lons + 2 * lons + lats + i, 1), :]
        ahead = jnp.where(row == lons - 1, east, pltpu.roll(value, lons - 1, 0))
        behind = jnp.where(row == 0, west, pltpu.roll(value, 1, 0))
        return ahead + behind

    if first:
        for n, half in enumerate(halves):
            field_ref, beyond_ref, around_ref = field_refs[n], field_refs[1 - n], around_refs[n]

            def masks(l, _, half=half, field_ref=field_ref, beyond_ref=beyond_ref, around_ref=around_ref):
                i = half * deep + l
                sea = field_ref[l]
                above = jnp.where(half == 0, rim_ref[5 * lons : 6 * lons, :], beyond_ref[deep - 1])
                below = jnp.where(half == 0, beyond_ref[0], rim_ref[4 * lons : 5 * lons, :])
                north = jnp.where(l == 0, above, field_ref[jnp.maximum(l - 1, 0)])
                south = jnp.where(l == deep - 1, below, field_ref[jnp.minimum(l + 1, deep - 1)])
                round_ = (north + south) + weight_ref[0, i] * beside(sea, i, 1)
                around_ref[l] = jnp.where(sea == 0.0, GAP, 1.0 - diffusion * round_)
                return _

            lax.fori_loop(0, deep, masks, 0, unroll=2)
            stores += fetch([(around_ref, out_hbm.at[pl.ds(n * deep, deep)])], out_sems.at[pl.ds(2 + n, 1)])

    wide_ref[...] = jnp.zeros_like(wide_ref)
    for n, half in enumerate(halves):

        def step(g, _, half=half, around_ref=around_refs[n], coded_ref=coded_refs[n]):
            smoothed = []
            for p in range(GROUP):
                l = g * GROUP + p
                i = half * deep + l
                around = around_ref[l]
                raw = pad_ref[i + 1]
                near = (pad_ref[i] + pad_ref[i + 2]) + weight_ref[0, i] * beside(raw, i, 0)
                smoothed.append(jnp.where(around == GAP, 0.0, around * raw + diffusion * near))
            spatial = times(split(jnp.concatenate(smoothed, axis=0)), inverse_side)
            parts = split(spatial)
            guess = times(parts, days_side)
            filled = []
            for p in range(GROUP):
                l = g * GROUP + p
                spatial_ref[half * deep + l] = spatial[p * lons : (p + 1) * lons]
                coded = coded_ref[l]
                filled.append(jnp.where(coded == GAP, guess[p * lons : (p + 1) * lons], coded))
            filled = split(jnp.concatenate(filled, axis=0))
            wide_ref[...] += dot_tn(jnp.concatenate([filled, parts], axis=1), parts)
            return _

        lax.fori_loop(0, deep // GROUP, step, 0)
        part = pl.ds(half * deep, deep)
        target = pl.ds(half * deep + (lats if first else 0), deep)
        stores += fetch([(spatial_ref.at[part], out_hbm.at[target])], out_sems.at[pl.ds(n, 1)])
    m = modes
    for part in range(2):
        at = 2 * part * m
        wide = wide_ref[at : at + m, :] + wide_ref[at + m : at + 2 * m, :]
        sums_ref[part * m : (part + 1) * m, :] = wide[:, :m] + wide[:, m:]
    for copy in stores:
        copy.wait()


def days_kernel(mine, core_ref, sums_ref, shelf_hbm, modes_hbm, ref, *refs):
    core = core_ref[0, 0]
    half = core if mine else 1 - core
    grid_ref, gram_ref, coded_ref, spatial_ref, sems = refs[-5:]
    lats, lons, modes = coded_ref.shape
    pairs = [(shelf_hbm.at[pl.ds(0, lats)], coded_ref), (modes_hbm.at[pl.ds((2 + half) * lats, lats)], spatial_ref)]
    loads = fetch(pairs, sems)
    spokes = ref.shape[0]
    many = DAYS_PIECES * lats // spokes
    if mine:
        temporal = sums_ref[...]
    else:
        days = sums_ref.shape[0] - modes
        temporal = full(sums_ref[0:days, :], inverse_spd(add_ridge(sums_ref[days:, :])))
        refs[0][...] = temporal
    side = right_side(temporal)
    across = right_side(temporal.T)
    gram_ref[...] = full(temporal, temporal, (((0,), (0,)), ((), ())))

    for copy in loads:
        copy.wait()

    def step(g, _):
        at = g * many
        guess = times(split(jnp.concatenate([spatial_ref[at + p] for p in range(many)], axis=0)), across)
        coded = jnp.concatenate([coded_ref[g * many + p] for p in range(many)], axis=0)
        put_rows(ref, grid_ref, g, g * many, times(split(jnp.where(coded == GAP, guess, coded)), side))
        return _

    lax.fori_loop(0, spokes // DAYS_PIECES, step, 0)
    put_block(half, grid_ref, gram_ref, ref)


def last_kernel(sums_ref, days_ref):
    days = days_ref.shape[0]
    days_ref[...] = full(sums_ref[0:days, :], inverse_spd(add_ridge(sums_ref[days:, :])))


SMEM = pl.BlockSpec(memory_space=pltpu.SMEM)
VMEM = pl.BlockSpec(memory_space=pltpu.VMEM)
HBM = pl.BlockSpec(memory_space=pltpu.HBM)


def call(kernel, outs, specs, scratch, name, flops, nbytes, room=60):
    return pl.pallas_call(
        kernel,
        out_shape=[jax.ShapeDtypeStruct(shape, f32) for shape, _ in outs],
        in_specs=specs,
        out_specs=[place for _, place in outs],
        scratch_shapes=[pltpu.VMEM(shape, f32) if isinstance(shape, tuple) else shape for shape in scratch],
        name=name,
        cost_estimate=pl.CostEstimate(flops=flops, bytes_accessed=nbytes, transcendentals=0),
        compiler_params=pltpu.CompilerParams(vmem_limit_bytes=room * 1024 * 1024),
    )


def copy_sems(count):
    return pltpu.SemaphoreType.DMA((count,))


def first_call(mine, core, anomaly, observed, mask, days, spokes):
    lats, lons, n = anomaly.shape
    block = (spokes, lats * lons // (2 * spokes) + 16, n)
    grid = (lats // 2, lons, n)
    scratch = [grid, (n, n), grid, pltpu.VMEM(grid, jnp.int32), pltpu.VMEM(mask.shape, jnp.int32), (n, n), grid, grid]
    scratch += [(lons, n), copy_sems(2 + 4 * (spokes // PIECES))]
    outs = [(block, VMEM), ((SHELF, lons, n), HBM)]
    specs = [SMEM] + [HBM] * 4
    return call(functools.partial(first_kernel, mine), outs, specs, scratch, "first_projection", 10**9, 10**7, FIRST_ROOM)(
        core, anomaly, observed, mask, days
    )


def modes_call(first, core, weight, here, there, days, shelves, lats):
    _, lons, n = shelves[0].shape
    half = (lats // 2, lons, n)
    grid = (lats, lons, n)
    outs = [((SHELF, lons, n) if first else grid, HBM), ((2 * n, n), VMEM)]
    scratch = [(lats + 2, lons, n), ((8 if first else 4) * lons, n), (4 * n, 2 * n), grid] + [half] * (6 if first else 4)
    scratch += [copy_sems(4), copy_sems(4)]
    specs = [SMEM, SMEM] + [VMEM] * 3 + [HBM] * len(shelves)
    return call(functools.partial(modes_kernel, first), outs, specs, scratch, "modes_sweep", 2 * 10**9, 10**7, ROOM)(
        core, weight, here, there, days, *shelves
    )


def days_call(mine, core, sums, shelf, modes, spokes, lats):
    _, lons, n = shelf.shape
    block = (spokes, lats * lons // (2 * spokes) + 16, n)
    outs = [(block, VMEM)] if mine else [(block, VMEM), ((sums.shape[0] - n, n), VMEM)]
    grid = (lats // 2, lons, n)
    scratch = [grid, (n, n), grid, grid, copy_sems(2)]
    return call(functools.partial(days_kernel, mine), outs, [SMEM, VMEM, HBM, HBM], scratch, "days_sweep", 2 * 10**9, 10**7, ROOM)(
        core, sums, shelf, modes
    )


def last_call(sums):
    n = sums.shape[1]
    return call(last_kernel, [((sums.shape[0] - n, n), VMEM)], [VMEM], [], "last_days", 10**7, 10**6, 16)(sums)[0]


def lat_weights(first_row, row_count, total_rows):
    index_rows = first_row + jnp.arange(row_count, dtype=jnp.float32)
    angle = (lat_south + lat_span * (index_rows + 0.5) / total_rows) * (math.pi / 180.0)
    cosine = jnp.cos(angle)
    return 1.0 / (cosine * cosine)


def swap_core(value):
    return lax.ppermute(value, "core", [(0, 1), (1, 0)])


def halo_pairs(lats, lons, spokes):
    pairs = []
    for la in range(lats):
        for lo in range(lons):
            for q in range(spokes):
                for core in range(2):
                    if q < spokes // 2:
                        to_la, to_lo = la + 2 * core - 1, lo
                    else:
                        to_la, to_lo = la, lo + (1 if q >= 3 * spokes // 4 else -1)
                    if 0 <= to_la < lats and 0 <= to_lo < lons:
                        here = ((la * lons + lo) * spokes + q) * 2 + core
                        there = ((to_la * lons + to_lo) * spokes + q) * 2 + core
                        pairs.append((here, there))
    return pairs


def gather_all(value, axes, size):
    spread = jnp.broadcast_to(value[None], (size,) + value.shape)
    return lax.all_to_all(spread, axes, 0, 0, tiled=True)


def sum_cells(value):
    size = lax.axis_size("lat") * lax.axis_size("lon")
    rows = value.shape[0]
    parts = lax.all_to_all(value.reshape(size, rows // size, -1), LL, 0, 0, tiled=True)
    mine = jnp.sum(parts, axis=0)
    return gather_all(mine, LL, size).reshape(rows, -1)


def edges_of(grid):
    middle = grid.shape[0] // 2
    up, down = grid[:middle], grid[middle:]
    return jnp.concatenate([up[0], up[:, 0], up[:, -1], down[-1], down[:, 0], down[:, -1]], axis=0)


def on_device(anomaly, observed, ocean_mask, start_days):
    rows_lat, cols_lon, _ = anomaly.shape
    rank_count = start_days.shape[1]
    lats, lons = lax.axis_size("lat"), lax.axis_size("lon")
    spokes = lax.axis_size("zlo") * lax.axis_size("y")
    core = lax.axis_index("core")
    spoke = lax.axis_index("zlo") * lax.axis_size("y") + lax.axis_index("y")
    pairs = halo_pairs(lats, lons, spokes)
    cells = rows_lat * cols_lon // (2 * spokes)
    core_word = core.reshape(1, 1).astype(jnp.int32)
    sea_grid = ocean_mask.astype(f32)
    first_lat = (lax.axis_index("lat") * rows_lat).astype(f32)
    weight = lat_weights(first_lat, rows_lat, float(rows_lat * lats)).reshape(1, rows_lat)
    edge_sea = lax.dynamic_slice_in_dim(edges_of(sea_grid), (core * spokes + spoke) * 8, 8)
    edge_sea = jnp.broadcast_to(edge_sea[:, None], (8, rank_count))
    temporal = start_days
    shelves = [None, None]
    other, shelves[1] = first_call(False, core_word, anomaly, observed, ocean_mask, start_days, spokes)
    mine, shelves[0] = first_call(True, core_word, anomaly, observed, ocean_mask, start_days, spokes)
    for sweep in range(ITERS):
        half = mine + swap_core(other)
        shard = jnp.sum(lax.all_to_all(half, YZ, 0, 0, tiled=True), axis=0)
        send = shard[cells : cells + 8]
        if sweep == 0:
            send = jnp.concatenate([send, edge_sea], axis=0)
        halo = lax.ppermute(send, ALL, pairs)
        shard = jnp.concatenate([shard[:cells], halo, shard[cells + 8 :]], axis=0)
        here = gather_all(shard, YZ, spokes)
        there = swap_core(here)
        spatial, sums = modes_call(sweep == 0, core_word, weight, here, there, temporal, shelves, rows_lat)
        sums = sum_cells(sums)
        if sweep == 0:
            shelves.append(spatial)
        if sweep < ITERS - 1:
            other, temporal = days_call(False, core_word, sums, shelves[1], spatial, spokes, rows_lat)
            (mine,) = days_call(True, core_word, temporal, shelves[0], spatial, spokes, rows_lat)
        else:
            temporal = last_call(sums)
    return (spatial, temporal)


def solution(mesh):
    lats, lons, days = mesh.devices.shape
    fine = Mesh(mesh.devices.reshape(lats, lons, 2, days // 4, 2), ALL)
    in_specs = (P("lat", "lon", DAY), P("lat", "lon", DAY), P("lat", "lon"), P(DAY, None))
    out_specs = (P("lat", "lon", None), P(DAY, None))
    return jax.shard_map(
        on_device, mesh=fine, in_specs=in_specs, out_specs=out_specs, check_vma=False
    )
```
